256 devices in a mesh: crop: 32 (over y, z), proto: 8 (over x, core).
Axes of the slice: x: 4, y: 4, z: 8, core: 2. Of those that a mesh axis runs over, the one named last changes fastest.
Arguments:
- student_features: bfloat16 [12288, 256], P('crop'), may hold values from -0.5 to 0.5
- teacher_features: bfloat16 [12288, 256], P('crop'), may hold values from -0.5 to 0.5
- student_weight: bfloat16 [256, 65536], P(None, 'proto'), may hold values from -0.375 to 0.375
- teacher_weight: bfloat16 [256, 65536], P(None, 'proto'), may hold values from -0.5 to 0.5
Outputs:
- weight_grad: float32 [256, 65536], P('crop', 'proto')
- student_gradient: float32 [12288, 256], P('crop', 'proto')
The draws below stay inside these ranges and needn't reach their ends.
All inputs are finite; a program needn't handle non-finite values.
Results may differ from the reference program's by a relative error of at most 0.0058.
The reference program's roundings to bfloat16 on the way count: a program that leaves them out, or rounds other values in their place, can miss the bound.
Values sent between devices are 32-bit elements; how exact they have to be, the bound alone decides.
A program may use at most 128 MiB of HBM per device.

```python
import jax
import jax.numpy as jnp
from jax import lax

D = 256
PROTOS = 65536
BALANCE_STEPS = 3
CROPS = 12288
LOSS_SCALE = 4194304
N_PROTO = 8


def shared_centers(key):
    return jax.random.truncated_normal(key, -4.0, 4.0, (32, D), jnp.float32)


def draw_teacher_features(key, part):
    centers = shared_centers(key)
    key = jax.random.fold_in(key, 11)
    first_key, second_key, noise_key = jax.random.split(key, 3)
    first = jax.random.randint(first_key, (CROPS,), 0, centers.shape[0])
    second = jax.random.randint(second_key, (CROPS,), 0, centers.shape[0])
    labels = jnp.minimum(first, second)
    noise = jax.random.truncated_normal(noise_key, -4.0, 4.0, (CROPS, D), jnp.float32)
    return (0.0625 * (centers[labels] + noise)).astype(jnp.bfloat16)


def draw_teacher_weight(key, part):
    centers = shared_centers(key)
    key = jax.random.fold_in(key, 23)
    label_key, noise_key = jax.random.split(key, 2)
    labels = jax.random.randint(label_key, (PROTOS,), 0, centers.shape[0])
    noise = jax.random.truncated_normal(noise_key, -4.0, 4.0, (D, PROTOS), jnp.float32)
    return (0.0625 * (centers[labels].T + noise)).astype(jnp.bfloat16)


def with_spikes(values, stream_key, source, target, parts, factor):
    owner, partner = [(jnp.arange(values.shape[position]) // (values.shape[position] // parts)).reshape([-1 if axis == position else 1 for axis in range(values.ndim)]) for position in (source, target)]
    chosen = jax.random.permutation(stream_key, parts)[partner]
    strong = (owner == chosen) | (owner == (partner + parts // 2) % parts)
    return jnp.where(strong, factor * values, values)


def steps_of(own_key, shape, cuts, low, top_value):
    level, own = 1.0, jax.random.fold_in(own_key, 6)
    for axis_at, parts in cuts:
        heights = jnp.exp(jax.random.uniform(jax.random.fold_in(own, axis_at), (parts,), jnp.float32, low / len(cuts), top_value / len(cuts)))
        level = level * jnp.repeat(heights, shape[axis_at] // parts).reshape([-1 if axis == axis_at else 1 for axis in range(len(shape))])
    return level


def centred(own_key, extent, spread, limit, shards=(), held_as=jnp.bfloat16):
    result = jax.random.normal(own_key, extent, jnp.float32) * spread
    if len(shards) > 0:
        result = steps_of(own_key, extent, shards, -0.22, 0.18) * result
    return jnp.clip(result, min=-limit, max=limit).astype(held_as)


def gaussian_with(own_key, shape, width, limit, pieces, heavy, held_as=jnp.bfloat16):
    result = width * jax.random.normal(own_key, shape, jnp.float32)
    if pieces:
        result = result * steps_of(own_key, shape, pieces, -0.22, 0.18)
    return jnp.clip(with_spikes(result, jax.random.fold_in(own_key, 3), *heavy), -limit, limit).astype(held_as)


def setup_inputs(seed: int = 0) -> dict:
    arg_keys = jax.random.split(jax.random.key(seed), 5)
    student_features = gaussian_with(arg_keys[0], (CROPS, D), 0.0625, 0.5, ((0, 32),), (0, 1, 32, 2.75))
    teacher_features = draw_teacher_features(jax.random.fold_in(arg_keys[4], 71), 0)
    student_weight = centred(arg_keys[2], (D, PROTOS), D ** -0.5, 0.375, ((1, 8),))
    teacher_weight = draw_teacher_weight(jax.random.fold_in(arg_keys[4], 71), 0)
    return {"student_features": student_features, "teacher_features": teacher_features, "student_weight": student_weight, "teacher_weight": teacher_weight}


EPSILON = 1e-06
TEACHER_TEMP = 0.07
STUDENT_TEMP = 0.1

def unit_rows(features):
    wide = features.astype(jnp.float32)
    row_norms = jnp.sqrt(lax.optimization_barrier(jnp.sum(wide * wide, axis=1, keepdims=True)) + EPSILON)
    return (wide / row_norms, row_norms)

def unit_columns(weight):
    wide = weight.astype(jnp.float32)
    column_norm_values = jnp.sqrt(lax.optimization_barrier(jnp.sum(wide * wide, axis=0)) + EPSILON)
    return (wide / column_norm_values, column_norm_values)

def reference(student_features, teacher_features, student_weight, teacher_weight):
    block_count = N_PROTO
    block_cols = PROTOS // block_count
    t_unit, t_norms = unit_rows(teacher_features)
    t_bf = t_unit.astype(jnp.bfloat16)
    s_unit, s_norms = unit_rows(student_features)
    s_bf = s_unit.astype(jnp.bfloat16)
    tw_unit, tw_norms = unit_columns(teacher_weight)
    tw_bf = tw_unit.astype(jnp.bfloat16)
    sw_unit, sw_norms = unit_columns(student_weight)
    sw_bf = sw_unit.astype(jnp.bfloat16)

    def to_blocks(matrix):
        return matrix.reshape(matrix.shape[0], block_count, block_cols).transpose(1, 0, 2)
    tw_blocks = to_blocks(tw_bf)
    sw_blocks = to_blocks(sw_bf)
    su_blocks = to_blocks(sw_unit)
    sn_blocks = sw_norms.reshape(block_count, block_cols)

    def teacher_exp(w_block):
        return jnp.exp(jnp.dot(t_bf, w_block, preferred_element_type=jnp.float32) / TEACHER_TEMP)
    row_scale = jnp.ones((CROPS,), jnp.float32)
    col_scale = jnp.ones((block_count, block_cols), jnp.float32)
    for balance_iteration in range(BALANCE_STEPS):

        def column_block(w_block, scale_now=row_scale):
            return lax.optimization_barrier(jnp.sum(teacher_exp(w_block) * scale_now[:, None], axis=0))
        col_sums = lax.map(column_block, tw_blocks)
        col_scale = 1.0 / col_sums

        def add_rows(row_acc, inputs):
            w_block, scale_block = inputs
            return (row_acc + lax.optimization_barrier(jnp.sum(teacher_exp(w_block) * scale_block[None, :], axis=1)), None)
        row_sums, unused = lax.scan(add_rows, jnp.zeros((CROPS,), jnp.float32), (tw_blocks, col_scale))
        row_scale = 1.0 / row_sums

    def add_total(row_acc, w_block):
        cosine = jnp.dot(s_bf, w_block, preferred_element_type=jnp.float32)
        return (row_acc + lax.optimization_barrier(jnp.sum(jnp.exp(cosine / STUDENT_TEMP), axis=1)), None)
    row_total, unused = lax.scan(add_total, jnp.zeros((CROPS,), jnp.float32), sw_blocks)
    factor = LOSS_SCALE / (STUDENT_TEMP * CROPS)

    def backward_pass(feat_grad, inputs):
        tw_block, sw_block, unit_block, norm_block, scale_block = inputs
        targets = teacher_exp(tw_block) * row_scale[:, None] * scale_block[None, :]
        cosine = jnp.dot(s_bf, sw_block, preferred_element_type=jnp.float32)
        student_prob = jnp.exp(cosine / STUDENT_TEMP) / row_total[:, None]
        logit_grad = ((student_prob - targets) * factor).astype(jnp.bfloat16)
        weight_sum = lax.dot_general(s_bf, logit_grad, (((0,), (0,)), ((), ())), preferred_element_type=jnp.float32)
        inner_prod = lax.optimization_barrier(jnp.sum(sw_block.astype(jnp.float32) * weight_sum, axis=0))
        block_gradient = (weight_sum - unit_block * inner_prod[None, :]) / norm_block[None, :]
        feat_grad = feat_grad + lax.dot_general(logit_grad, sw_block, (((1,), (1,)), ((), ())), preferred_element_type=jnp.float32)
        return (feat_grad, block_gradient)
    feat_grad, grad_blocks = lax.scan(backward_pass, jnp.zeros((CROPS, D), jnp.float32), (tw_blocks, sw_blocks, su_blocks, sn_blocks, col_scale))
    weight_grad = grad_blocks.transpose(1, 0, 2).reshape(D, PROTOS)
    inner_row_block = lax.optimization_barrier(jnp.sum(s_bf.astype(jnp.float32) * feat_grad, axis=1))
    student_gradient = (feat_grad - s_unit * inner_row_block[:, None]) / s_norms
    return (weight_grad, student_gradient)
```

```python
import functools
import math

import jax
import jax.numpy as jnp
from jax import lax
from jax.experimental import pallas as pl
from jax.experimental.pallas import tpu as pltpu
from jax.sharding import PartitionSpec as P

BALANCE_STEPS = 3
LOSS_SCALE = 4194304
EPSILON = 1e-06
TEACHER_TEMP = 0.07
STUDENT_TEMP = 0.1
LOG2E = math.log2(math.e)

NY, NZ, NX, NC = 4, 8, 4, 2
D = 256
ROWS = 384
TILE_ROWS = NY * ROWS
TILE_COLS = 2048
HALF = TILE_COLS // 2
QUARTER = TILE_COLS // 4
BLOCKS = TILE_ROWS // 128
MESH = pl.DeviceIdType.MESH
F32, BF16 = jnp.float32, jnp.bfloat16


def kernel(
    factor,
    t_ref, s_ref, tw_hbm, sw_hbm,
    wout_ref, hout_ref,
    E, A, tw_raw, sw_raw, tw_bf, sw_bf, sw_t, sw_inv, t_bf, s_bf, s_t, s_unit, s_inv,
    u_wide, z_wide, t_src, s_src, t_in, s_in,
    c_src, c_in, r_src, r_in, z_src, z_in, v_ref,
    L, G, ring_r, ring_l, g_sum, g_out, H, HT, h_core, h_in,
    load_sem, t_send, t_recv, t_fsend, t_frecv, s_send, s_recv, s_fsend, s_frecv,
    c_send, c_recv, r_send, r_recv, z_send, z_recv,
    rr_send, rr_recv, rl_send, rl_recv, a_send, a_recv, hc_send, hc_recv, h_send, h_recv,
):
    crop, proto = lax.axis_index("crop"), lax.axis_index("proto")
    y, z, x, c = crop // NZ, crop % NZ, proto // NC, proto % NC

    def dev(dy, dz, dx, dc):
        return (((y + dy) % NY) * NZ + (z + dz) % NZ, ((x + dx) % NX) * NC + (c + dc) % NC)

    def remote(src, dst, send, recv, to):
        return pltpu.make_async_remote_copy(
            src_ref=src, dst_ref=dst, send_sem=send, recv_sem=recv, device_id=to, device_id_type=MESH
        )

    def wait_bytes(buf, sem):
        pltpu.make_async_copy(buf, buf, sem).wait()

    plane = [
        (dy, dx, dc) for dy in range(NY) for dx in range(NX) for dc in range(NC) if (dy, dx, dc) != (0, 0, 0)
    ]
    sheet = [(dy, dx) for dy in range(NY) for dx in range(NX) if (dy, dx) != (0, 0)]

    barrier = pltpu.get_barrier_semaphore()
    for dy, dx, dc in plane:
        pl.semaphore_signal(barrier, inc=1, device_id=dev(dy, 0, dx, dc), device_id_type=MESH)
    for dz in range(1, NZ):
        pl.semaphore_signal(barrier, inc=1, device_id=dev(0, dz, 0, 0), device_id_type=MESH)

    col0 = pl.multiple_of(y * TILE_COLS, TILE_COLS)
    load_t = pltpu.make_async_copy(tw_hbm.at[:, pl.ds(col0, TILE_COLS)], tw_raw, load_sem.at[0])
    load_s = pltpu.make_async_copy(sw_hbm.at[:, pl.ds(col0, TILE_COLS)], sw_raw, load_sem.at[1])
    load_t.start()
    load_s.start()

    def block_rows(block):
        return pl.ds(pl.multiple_of(block * ROWS, ROWS), ROWS)

    t32 = t_ref[...].astype(F32)
    t_own = (t32 * (1.0 / jnp.sqrt(jnp.sum(t32 * t32, axis=1, keepdims=True) + EPSILON))).astype(BF16)
    t_bf[block_rows(y), :] = t_own
    t_src[...] = t_own.astype(F32).reshape(2, ROWS // 2, D)
    s_src[...] = s_ref[...].astype(F32).reshape(2, ROWS // 2, D)

    pl.semaphore_wait(barrier, len(plane) + NZ - 1)

    def gather_start(src, dst, send, recv):
        for o in (1, 3, 2):
            remote(src.at[c], dst.at[o - 1, c], send, recv.at[o - 1], dev(o, 0, 0, 0)).start()

    def gather_forward(dst, recv, fsend, frecv, o):
        wait_bytes(dst.at[o - 1, c], recv.at[o - 1])
        remote(dst.at[o - 1, c], dst.at[o - 1, c], fsend, frecv.at[o - 1], dev(0, 0, 0, 1)).start()

    gather_start(t_src, t_in, t_send, t_recv)

    load_t.wait()

    def normalise(q, carry, raw, out, inv_ref):
        cols = pl.ds(pl.multiple_of(q * QUARTER, QUARTER), QUARTER)
        w = raw[:, cols].astype(F32)
        inv = 1.0 / jnp.sqrt(jnp.sum(w * w, axis=0, keepdims=True) + EPSILON)
        out[:, cols] = (w * inv).astype(BF16)
        if inv_ref is not None:
            inv_ref[:, cols] = inv
        return carry

    lax.fori_loop(0, 4, functools.partial(normalise, raw=tw_raw, out=tw_bf, inv_ref=None), 0)

    def exp_block(block, first):
        rows = block_rows(block)

        def one(q, carry):
            cols = pl.ds(pl.multiple_of(q * QUARTER, QUARTER), QUARTER)
            e = jnp.exp2(
                jnp.dot(t_bf[rows, :], tw_bf[:, cols], preferred_element_type=F32) * (LOG2E / TEACHER_TEMP)
            )
            E[rows, cols] = e
            part = jnp.sum(e.reshape(ROWS // 8, 8, QUARTER), axis=0)
            c_acc = part if first else part + v_ref[:, cols]
            v_ref[:, cols] = c_acc
            return carry

        lax.fori_loop(0, 4, one, 0)

    exp_block(y, True)
    load_s.wait()
    lax.fori_loop(0, 4, functools.partial(normalise, raw=sw_raw, out=sw_bf, inv_ref=sw_inv), 0)
    for o in (1, 3, 2):
        gather_forward(t_in, t_recv, t_fsend, t_frecv, o)
    gather_start(s_src, s_in, s_send, s_recv)
    for o in (1, 3, 2):
        wait_bytes(t_in.at[o - 1, 1 - c], t_frecv.at[o - 1])
        block = (y + NY - o) % NY
        t_bf[block_rows(block), :] = t_in[o - 1].reshape(ROWS, D).astype(BF16)
        exp_block(block, False)

    def cols_start(r, sums):
        c_src[r] = jnp.sum(sums, axis=0, keepdims=True)
        for dz in range(1, NZ):
            remote(c_src.at[r], c_in.at[r, dz - 1], c_send.at[r], c_recv.at[r], dev(0, dz, 0, 0)).start()

    def cols_done(r):
        wait_bytes(c_in.at[r], c_recv.at[r])
        total = c_src[r]
        for dz in range(1, NZ):
            total = total + c_in[r, dz - 1]
        return 1.0 / total

    def rows_of(src, dst, scale):
        def one(b, carry):
            rows = pl.ds(pl.multiple_of(b * 128, 128), 128)
            acc = None
            for k in range(TILE_COLS // 128):
                term = src[rows, k * 128:(k + 1) * 128]
                if scale is not None:
                    term = term * scale[:, k * 128:(k + 1) * 128]
                acc = term if acc is None else acc + term
            dst[pl.ds(b, 1), :] = jnp.sum(acc.T, axis=0, keepdims=True)
            return carry

        lax.fori_loop(0, BLOCKS, one, 0)

    def rows_start(src, dst, send, recv):
        for i, (dy, dx, dc) in enumerate(plane):
            remote(src, dst.at[i], send, recv, dev(dy, 0, dx, dc)).start()

    def rows_done(src, dst, recv):
        wait_bytes(dst, recv)
        total = src[...]
        for i in range(len(plane)):
            total = total + dst[i]
        return 1.0 / total

    def widen(dst, flat):
        for b in range(BLOCKS):
            dst[b * 128:(b + 1) * 128, :] = jnp.broadcast_to(flat[b:b + 1, :], (128, 128)).T

    def cols_of():
        def one(b, acc):
            rows = pl.ds(pl.multiple_of(b * 128, 128), 128)
            u = u_wide[rows, :]
            out = []
            for k in range(TILE_COLS // 128):
                e = E[rows, k * 128:(k + 1) * 128] * u
                out.append(acc[k] + jnp.sum(e.reshape(16, 8, 128), axis=0))
            return tuple(out)

        zero = tuple(jnp.zeros((8, 128), F32) for _ in range(TILE_COLS // 128))
        acc = lax.fori_loop(0, BLOCKS, one, zero)
        return jnp.concatenate(acc, axis=1)

    def student_exp(b0, b1):
        def one(i, carry):
            b, q = i // 4, i % 4
            rows = pl.ds(pl.multiple_of(b * ROWS, ROWS), ROWS)
            cols = pl.ds(pl.multiple_of(q * QUARTER, QUARTER), QUARTER)
            A[rows, cols] = jnp.exp2(
                jnp.dot(s_bf[rows, :], sw_bf[:, cols], preferred_element_type=F32) * (LOG2E / STUDENT_TEMP)
            )
            return carry

        lax.fori_loop(b0 * 4, b1 * 4, one, 0)

    def student_block(block, raw):
        inv = 1.0 / jnp.sqrt(jnp.sum(raw * raw, axis=1, keepdims=True) + EPSILON)
        unit = raw * inv
        rows = block_rows(block)
        s_unit[rows, :] = unit
        s_inv[rows, :] = jnp.broadcast_to(inv, (ROWS, 128))
        s_bf[rows, :] = unit.astype(BF16)

    cols_start(0, v_ref[...])
    student_block(y, s_src[...].reshape(ROWS, D))
    for q in range(4):
        sw_t[q * QUARTER:(q + 1) * QUARTER, :] = sw_bf[:, q * QUARTER:(q + 1) * QUARTER].T
    v = cols_done(0)
    rows_of(E, r_src.at[0], v)
    rows_start(r_src.at[0], r_in.at[0], r_send.at[0], r_recv.at[0])
    for o in (1, 3, 2):
        gather_forward(s_in, s_recv, s_fsend, s_frecv, o)
    widen(u_wide, rows_done(r_src.at[0], r_in.at[0], r_recv.at[0]))
    cols_start(1, cols_of())
    for o in (1, 3, 2):
        wait_bytes(s_in.at[o - 1, 1 - c], s_frecv.at[o - 1])
        student_block((y + NY - o) % NY, s_in[o - 1].reshape(ROWS, D))
    v = cols_done(1)
    rows_of(E, r_src.at[1], v)
    rows_start(r_src.at[1], r_in.at[1], r_send.at[1], r_recv.at[1])
    student_exp(0, 3)
    widen(u_wide, rows_done(r_src.at[1], r_in.at[1], r_recv.at[1]))
    cols_start(2, cols_of())
    student_exp(3, 4)
    rows_of(A, z_src, None)
    v = cols_done(2)
    v_ref[0:1, :] = v
    rows_of(E, r_src.at[2], v)
    rows_start(r_src.at[2], r_in.at[2], r_send.at[2], r_recv.at[2])
    rows_start(z_src, z_in, z_send, z_recv)
    for b in range(BLOCKS):
        s_t[:, b * 128:(b + 1) * 128] = s_bf[b * 128:(b + 1) * 128, :].T
    widen(z_wide, rows_done(z_src, z_in, z_recv) * factor)
    widen(u_wide, rows_done(r_src.at[2], r_in.at[2], r_recv.at[2]) * factor)

    def quarter(q):
        lo = q * QUARTER

        def one(b, carry):
            rows = pl.ds(pl.multiple_of(b * 128, 128), 128)
            u, w = u_wide[rows, :], z_wide[rows, :]
            for k in range(QUARTER // 128):
                at = slice(lo + k * 128, lo + (k + 1) * 128)
                grad = A[rows, at] * w - E[rows, at] * u * v_ref[0:1, at]
                L[rows, k * 128:(k + 1) * 128] = grad.astype(BF16)
            return carry

        lax.fori_loop(0, BLOCKS, one, 0)
        cols = slice(lo, lo + QUARTER)
        g = jnp.dot(s_t[...], L[...], preferred_element_type=F32)
        inv = sw_inv[:, cols]
        inner = jnp.sum(sw_bf[:, cols].astype(F32) * g, axis=0, keepdims=True)
        g = (g - sw_raw[:, cols].astype(F32) * (inv * inner)) * inv
        at = (q % 2) * QUARTER
        G[q // 2, :, :, :, at:at + QUARTER] = g.reshape(NY, NZ, 8, QUARTER)
        def rows_h(b, carry):
            rows = pl.ds(pl.multiple_of(b * ROWS, ROWS), ROWS)
            h = jnp.dot(L[rows, :], sw_t[cols, :], preferred_element_type=F32)
            H[rows, :] = h if q == 0 else H[rows, :] + h
            return carry

        lax.fori_loop(0, NY, rows_h, 0)

    def ring(i, buf, send, recv, way):
        half = i % 2 if way == 1 else 1 - i % 2
        hops = NZ // 2 - (i + 1) // 2
        dest = (z + way * hops + NZ) % NZ
        if i < 2:
            src = G.at[half, :, dest]
        else:
            wait_bytes(buf.at[i - 2], recv.at[i - 2])
            buf[i - 2] = buf[i - 2] + G[half, :, dest]
            src = buf.at[i - 2]
        remote(src, buf.at[i], send.at[i], recv.at[i], dev(0, way, 0, 0)).start()

    def ring_right(i):
        ring(i, ring_r, rr_send, rr_recv, 1)

    def ring_left(i):
        ring(i, ring_l, rl_send, rl_recv, -1)

    quarter(0)
    quarter(1)
    ring_right(0)
    quarter(2)
    quarter(3)
    ring_left(0)
    ring_right(1)
    ring_left(1)

    def finish_h(b, carry):
        rows = pl.ds(pl.multiple_of(b * 128, 128), 128)
        h = H[rows, :]
        inner = jnp.sum(s_bf[rows, :].astype(F32) * h, axis=1, keepdims=True)
        inv = s_inv[rows, :]
        h = (h - s_unit[rows, :] * inner) * jnp.concatenate([inv, inv], axis=1)
        turned = h.T
        for p in range(NX * NC):
            HT[p % NC, p // NC, :, rows] = turned[p * 32:(p + 1) * 32, :]
        return carry

    lax.fori_loop(0, BLOCKS, finish_h, 0)
    core = remote(HT.at[1 - c], h_core, hc_send, hc_recv, dev(0, 0, 0, 1))
    core.start()
    ring_right(2)
    ring_left(2)
    core.wait_recv()

    def add_h(i, carry):
        HT[c, i] = HT[c, i] + h_core[i]
        return carry

    lax.fori_loop(0, NX, add_h, 0)
    for i, (dy, dx) in enumerate(sheet):
        to_y, to_x = (y + dy) % NY, (x + dx) % NX
        remote(
            HT.at[c, to_x, :, block_rows(to_y)], h_in.at[i], h_send, h_recv, dev(dy, 0, dx, 0)
        ).start()
    for i in range(3, 7):
        ring_right(i)
        ring_left(i)

    wait_bytes(h_in, h_recv)
    total = HT[c, x, :, block_rows(y)]
    for i in range(len(sheet)):
        total = total + h_in[i]
    hout_ref[...] = total

    def turn(half, last_r, last_l):
        wait_bytes(ring_r.at[last_r], rr_recv.at[last_r])
        wait_bytes(ring_l.at[last_l], rl_recv.at[last_l])
        g_sum[half] = G[half, :, z] + ring_r[last_r] + ring_l[last_l]
        for o in range(1, NY):
            remote(
                g_sum.at[half, (y + o) % NY], g_out.at[half, o - 1], a_send.at[half], a_recv.at[half], dev(o, 0, 0, 0)
            ).start()
        wout_ref[:, pl.ds(pl.multiple_of(y * TILE_COLS + half * HALF, HALF), HALF)] = g_sum[half, y]

    turn(0, 6, 5)
    turn(1, 5, 6)
    for half in range(2):
        wait_bytes(g_out.at[half], a_recv.at[half])
        for o in range(1, NY):
            at = pl.multiple_of(((y + NY - o) % NY) * TILE_COLS + half * HALF, HALF)
            wout_ref[:, pl.ds(at, HALF)] = g_out[half, o - 1]

    wait_bytes(t_in.at[:, 0], t_send)
    wait_bytes(t_in.at[:, 0], t_fsend)
    wait_bytes(s_in.at[:, 0], s_send)
    wait_bytes(s_in.at[:, 0], s_fsend)
    for r in range(BALANCE_STEPS):
        wait_bytes(c_in.at[r], c_send.at[r])
        wait_bytes(r_in.at[r], r_send.at[r])
    wait_bytes(z_in, z_send)
    for i in range(7):
        wait_bytes(ring_r.at[i], rr_send.at[i])
        wait_bytes(ring_l.at[i], rl_send.at[i])
    core.wait_send()
    wait_bytes(h_in, h_send)
    for half in range(2):
        wait_bytes(g_out.at[half], a_send.at[half])


def shards(student_features, teacher_features, student_weight, teacher_weight):
    crops_all = student_features.shape[0] * lax.axis_size("crop")
    factor = LOSS_SCALE / (STUDENT_TEMP * crops_all)
    vmem = pl.BlockSpec(memory_space=pltpu.VMEM)
    hbm = pl.BlockSpec(memory_space=pl.ANY)
    peers, sheet = NY * NX * NC - 1, NY * NX - 1
    v = pltpu.VMEM
    dma = pltpu.SemaphoreType.DMA
    scratch = [
        v((TILE_ROWS, TILE_COLS), F32), v((TILE_ROWS, TILE_COLS), F32),
        v((D, TILE_COLS), BF16), v((D, TILE_COLS), BF16),
        v((D, TILE_COLS), BF16), v((D, TILE_COLS), BF16),
        v((TILE_COLS, D), BF16), v((1, TILE_COLS), F32),
        v((TILE_ROWS, D), BF16), v((TILE_ROWS, D), BF16), v((D, TILE_ROWS), BF16),
        v((TILE_ROWS, D), F32), v((TILE_ROWS, 128), F32),
        v((TILE_ROWS, 128), F32), v((TILE_ROWS, 128), F32),
        v((2, ROWS // 2, D), F32), v((2, ROWS // 2, D), F32),
        v((NY - 1, 2, ROWS // 2, D), F32), v((NY - 1, 2, ROWS // 2, D), F32),
        v((BALANCE_STEPS, 1, TILE_COLS), F32), v((BALANCE_STEPS, NZ - 1, 1, TILE_COLS), F32),
        v((BALANCE_STEPS, BLOCKS, 128), F32), v((BALANCE_STEPS, peers, BLOCKS, 128), F32),
        v((BLOCKS, 128), F32), v((peers, BLOCKS, 128), F32),
        v((8, TILE_COLS), F32),
        v((TILE_ROWS, QUARTER), BF16),
        v((2, NY, NZ, 8, HALF), F32),
        v((7, NY, 8, HALF), F32), v((7, NY, 8, HALF), F32),
        v((2, NY, 8, HALF), F32), v((2, NY - 1, 8, HALF), F32),
        v((TILE_ROWS, D), F32), v((NC, NX, 32, TILE_ROWS), F32),
        v((NX, 32, TILE_ROWS), F32), v((sheet, 32, ROWS), F32),
        dma((2,)),
        dma, dma((3,)), dma, dma((3,)),
        dma, dma((3,)), dma, dma((3,)),
        dma((3,)), dma((3,)), dma((3,)), dma((3,)), dma, dma,
        dma((7,)), dma((7,)), dma((7,)), dma((7,)),
        dma((2,)), dma((2,)), dma, dma, dma, dma,
    ]
    weight_grad, turned = pl.pallas_call(
        functools.partial(kernel, factor),
        out_shape=(
            jax.ShapeDtypeStruct((D // (NY * NZ), NY * TILE_COLS), F32),
            jax.ShapeDtypeStruct((D // (NX * NC), ROWS), F32),
        ),
        in_specs=[vmem, vmem, hbm, hbm],
        out_specs=(vmem, vmem),
        scratch_shapes=scratch,
        compiler_params=pltpu.CompilerParams(
            collective_id=0, has_side_effects=True, vmem_limit_bytes=60 * 1024 * 1024
        ),
        name="prototype_head",
    )(teacher_features, student_features, teacher_weight, student_weight)
    return weight_grad, turned.T


def solution(mesh):
    return jax.shard_map(
        shards,
        mesh=mesh,
        in_specs=(P("crop", None), P("crop", None), P(None, "proto"), P(None, "proto")),
        out_specs=(P("crop", "proto"), P("crop", "proto")),
        check_vma=False,
    )
```

```python
import functools
import math

import jax
import jax.numpy as jnp
from jax import lax
from jax.experimental import pallas as pl
from jax.experimental.pallas import tpu as pltpu
from jax.sharding import PartitionSpec as P

BALANCE_STEPS = 3
LOSS_SCALE = 4194304
EPSILON = 1e-06
TEACHER_TEMP = 0.07
STUDENT_TEMP = 0.1
LOG2E = math.log2(math.e)

NY, NZ, NX, NC = 4, 8, 4, 2
D = 256
ROWS = 384
TILE_ROWS = NY * ROWS
TILE_COLS = 2048
HALF = TILE_COLS // 2
QUARTER = TILE_COLS // 4
BLOCKS = TILE_ROWS // 128
PIECE = ROWS // 4
MESH = pl.DeviceIdType.MESH
F32, BF16 = jnp.float32, jnp.bfloat16


def kernel(
    factor,
    t_ref, s_ref, tw_hbm, sw_hbm,
    wout_ref, hout_ref,
    E, A, tw_raw, sw_raw, tw_bf, sw_bf, sw_t, sw_inv, t_bf, s_bf, s_t, s_raw, s_inv,
    u_wide, part, t_src, s_src, t_in, s_in,
    c_src, c_in, r_src, r_in, flat_ref, v_ref,
    L, G, ring_r, ring_l, g_sum, g_out, h_core, h_in,
    load_sem, t_send, t_recv, t_fsend, t_frecv, s_send, s_recv, s_fsend, s_frecv,
    c_send, c_recv, r_send, r_recv,
    rr_send, rr_recv, rl_send, rl_recv, a_send, a_recv, hc_send, hc_recv, h_send, h_recv,
):
    crop, proto = lax.axis_index("crop"), lax.axis_index("proto")
    y, z, x, c = crop // NZ, crop % NZ, proto // NC, proto % NC

    def dev(dy, dz, dx, dc):
        return (((y + dy) % NY) * NZ + (z + dz) % NZ, ((x + dx) % NX) * NC + (c + dc) % NC)

    def remote(src, dst, send, recv, to):
        return pltpu.make_async_remote_copy(
            src_ref=src, dst_ref=dst, send_sem=send, recv_sem=recv, device_id=to, device_id_type=MESH
        )

    def wait_bytes(buf, sem):
        pltpu.make_async_copy(buf, buf, sem).wait()

    def far(d, n):
        return min(d, n - d)

    plane = sorted(
        ((dy, dx, dc) for dy in range(NY) for dx in range(NX) for dc in range(NC) if (dy, dx, dc) != (0, 0, 0)),
        key=lambda o: -(far(o[0], NY) + far(o[1], NX)),
    )
    sheet = sorted(
        ((dy, dx) for dy in range(NY) for dx in range(NX) if (dy, dx) != (0, 0)),
        key=lambda o: -(far(o[0], NY) + far(o[1], NX)),
    )
    line = sorted(range(1, NZ), key=lambda d: -far(d, NZ))

    barrier = pltpu.get_barrier_semaphore()
    for dy, dx, dc in plane:
        pl.semaphore_signal(barrier, inc=1, device_id=dev(dy, 0, dx, dc), device_id_type=MESH)
    for dz in line:
        pl.semaphore_signal(barrier, inc=1, device_id=dev(0, dz, 0, 0), device_id_type=MESH)

    col0 = pl.multiple_of(y * TILE_COLS, TILE_COLS)
    load_t = pltpu.make_async_copy(tw_hbm.at[:, pl.ds(col0, TILE_COLS)], tw_raw, load_sem.at[0])
    load_s = pltpu.make_async_copy(sw_hbm.at[:, pl.ds(col0, TILE_COLS)], sw_raw, load_sem.at[1])
    load_t.start()
    load_s.start()

    def block_rows(block):
        return pl.ds(pl.multiple_of(block * ROWS, ROWS), ROWS)

    def normalise(raw, out, inv_ref):
        def one(q, carry):
            cols = pl.ds(pl.multiple_of(q * QUARTER, QUARTER), QUARTER)
            w = raw[:, cols].astype(F32)
            inv = 1.0 / jnp.sqrt(jnp.sum(w * w, axis=0, keepdims=True) + EPSILON)
            out[:, cols] = (w * inv).astype(BF16)
            if inv_ref is not None:
                inv_ref[:, cols] = inv
            return carry

        lax.fori_loop(0, 4, one, 0)

    t32 = t_ref[...].astype(F32)
    t_own = (t32 * (1.0 / jnp.sqrt(jnp.sum(t32 * t32, axis=1, keepdims=True) + EPSILON))).astype(BF16)
    t_bf[block_rows(y), :] = t_own
    t_src[...] = t_own.astype(F32).reshape(2, 2, PIECE, D)
    s_src[...] = s_ref[...].astype(F32).reshape(2, 2, PIECE, D)

    pl.semaphore_wait(barrier, len(plane) + NZ - 1)

    def gather_start(src, dst, send, recv):
        for piece, way in ((0, 1), (1, 3), (1, 1), (0, 3)):
            remote(src.at[c, piece], dst.at[way - 1, c, piece], send, recv.at[way - 1, piece], dev(way, 0, 0, 0)).start()

    def gather_relay(dst, send, recv):
        for piece, way in ((0, 1), (1, 3)):
            wait_bytes(dst.at[way - 1, c, piece], recv.at[way - 1, piece])
            remote(
                dst.at[way - 1, c, piece], dst.at[1, c, piece], send, recv.at[1, piece], dev(way, 0, 0, 0)
            ).start()

    def gather_core(dst, fsend, frecv, way, piece):
        remote(
            dst.at[way - 1, c, piece], dst.at[way - 1, c, piece], fsend, frecv.at[way - 1, piece], dev(0, 0, 0, 1)
        ).start()

    def gather_near(dst, recv, fsend, frecv):
        gather_core(dst, fsend, frecv, 1, 0)
        gather_core(dst, fsend, frecv, 3, 1)
        for piece, way in ((1, 1), (0, 3)):
            wait_bytes(dst.at[way - 1, c, piece], recv.at[way - 1, piece])
            gather_core(dst, fsend, frecv, way, piece)

    def gather_far(dst, recv, fsend, frecv):
        for piece in range(2):
            wait_bytes(dst.at[1, c, piece], recv.at[1, piece])
            gather_core(dst, fsend, frecv, 2, piece)

    def gather_done(dst, frecv, way):
        for piece in range(2):
            wait_bytes(dst.at[way - 1, 1 - c, piece], frecv.at[way - 1, piece])
        return (y + NY - way) % NY, dst[way - 1].reshape(ROWS, D)

    gather_start(t_src, t_in, t_send, t_recv)
    load_t.wait()
    normalise(tw_raw, tw_bf, None)

    def exp_block(block, first):
        rows = block_rows(block)

        def one(q, carry):
            cols = pl.ds(pl.multiple_of(q * HALF, HALF), HALF)
            e = jnp.exp2(
                jnp.dot(t_bf[rows, :], tw_bf[:, cols], preferred_element_type=F32) * (LOG2E / TEACHER_TEMP)
            )
            E[rows, cols] = e
            sums = jnp.sum(e.reshape(ROWS // 8, 8, HALF), axis=0)
            v_ref[:, cols] = sums if first else sums + v_ref[:, cols]
            return carry

        lax.fori_loop(0, 2, one, 0)

    exp_block(y, True)
    gather_relay(t_in, t_send, t_recv)
    load_s.wait()
    normalise(sw_raw, sw_bf, sw_inv)
    gather_near(t_in, t_recv, t_fsend, t_frecv)
    for way in (1, 3, 2):
        if way == 3:
            gather_far(t_in, t_recv, t_fsend, t_frecv)
        block, rows = gather_done(t_in, t_frecv, way)
        t_bf[block_rows(block), :] = rows.astype(BF16)
        exp_block(block, False)

    def cols_start(r, sums):
        c_src[r] = jnp.sum(sums, axis=0, keepdims=True)
        for i, dz in enumerate(line):
            remote(c_src.at[r], c_in.at[r, i], c_send.at[r], c_recv.at[r], dev(0, dz, 0, 0)).start()

    def cols_done(r):
        wait_bytes(c_in.at[r], c_recv.at[r])
        total = c_src[r]
        for i in range(len(line)):
            total = total + c_in[r, i]
        return 1.0 / total

    lane = lax.broadcasted_iota(jnp.int32, (8, 128), 1)
    sublane = lax.broadcasted_iota(jnp.int32, (8, 128), 0)

    def rows_of(src, r, scale, store):
        def one(b, carry):
            rows = pl.ds(pl.multiple_of(b * 128, 128), 128)
            acc = None
            for k in range(TILE_COLS // 128):
                cols = slice(k * 128, (k + 1) * 128)
                term = src[rows, cols]
                if scale is not None:
                    term = term * scale[:, cols]
                if store:
                    src[rows, cols] = term
                acc = term if acc is None else acc + term
            part[rows, :] = acc
            return carry

        lax.fori_loop(0, BLOCKS, one, 0)

        def packed(g0, g1):
            out = None
            for base in range(g0, g1, 16):
                some = jnp.zeros((8, 128), F32)
                for g in range(base, base + 16):
                    total = jnp.sum(part[8 * g:8 * g + 8, :], axis=1, keepdims=True)
                    some = jnp.where(lane == g - g0, total, some)
                out = some if out is None else out + some
            return out

        r_src[r, 0:8, :] = packed(0, 128)
        rest = packed(128, 192)
        rest = rest + pltpu.roll(pltpu.roll(rest, 64, 1), 4, 0)
        r_src[r, 8:12, :] = rest[0:4, :]

    def rows_start(r):
        for i, (dy, dx, dc) in enumerate(plane):
            remote(r_src.at[r], r_in.at[r, i], r_send.at[r], r_recv.at[r], dev(dy, 0, dx, dc)).start()

    def rows_done(r, dst, scale):
        wait_bytes(r_in.at[r], r_recv.at[r])
        total = r_src[r]
        for i in range(len(plane)):
            total = total + r_in[r, i]
        flat_ref[0:BLOCKS, :] = scale / total
        low, rest = flat_ref[0:8, :], flat_ref[8:16, :]
        high = jnp.where(sublane < 4, rest, pltpu.roll(pltpu.roll(rest, 64, 1), 4, 0))
        for g in range(TILE_ROWS // 8):
            value = low[:, g:g + 1] if g < 128 else high[:, g - 128:g - 127]
            dst[8 * g:8 * g + 8, :] = jnp.broadcast_to(value, (8, 128))

    def cols_of():
        def one(b, acc):
            rows = pl.ds(pl.multiple_of(b * 128, 128), 128)
            u = u_wide[rows, :]
            out = []
            for k in range(TILE_COLS // 128):
                e = E[rows, k * 128:(k + 1) * 128] * u
                out.append(acc[k] + jnp.sum(e.reshape(16, 8, 128), axis=0))
            return tuple(out)

        zero = tuple(jnp.zeros((8, 128), F32) for _ in range(TILE_COLS // 128))
        acc = lax.fori_loop(0, BLOCKS, one, zero)
        return jnp.concatenate(acc, axis=1)

    def student_exp():
        def one(i, carry):
            rows = pl.ds(pl.multiple_of((i // 2) * ROWS, ROWS), ROWS)
            cols = pl.ds(pl.multiple_of((i % 2) * HALF, HALF), HALF)
            A[rows, cols] = jnp.exp2(
                jnp.dot(s_bf[rows, :], sw_bf[:, cols], preferred_element_type=F32) * (LOG2E / STUDENT_TEMP)
            )
            return carry

        lax.fori_loop(0, 2 * NY, one, 0)

    def student_block(block, raw):
        inv = 1.0 / jnp.sqrt(jnp.sum(raw * raw, axis=1, keepdims=True) + EPSILON)
        unit = raw * inv
        rows = block_rows(block)
        s_raw[rows, :] = raw.astype(BF16)
        s_inv[rows, :] = jnp.broadcast_to(inv, (ROWS, 128))
        s_bf[rows, :] = unit.astype(BF16)

    cols_start(0, v_ref[...])
    gather_start(s_src, s_in, s_send, s_recv)
    student_block(y, s_src[...].reshape(ROWS, D))
    for q in range(4):
        sw_t[q * QUARTER:(q + 1) * QUARTER, :] = sw_bf[:, q * QUARTER:(q + 1) * QUARTER].T
    v = cols_done(0)
    rows_of(E, 0, v, False)
    rows_start(0)
    gather_relay(s_in, s_send, s_recv)
    gather_near(s_in, s_recv, s_fsend, s_frecv)
    rows_done(0, u_wide, 1.0)
    cols_start(1, cols_of())
    gather_far(s_in, s_recv, s_fsend, s_frecv)
    for way in (1, 3, 2):
        student_block(*gather_done(s_in, s_frecv, way))
    v = cols_done(1)
    rows_of(E, 1, v, False)
    rows_start(1)
    student_exp()
    rows_done(1, u_wide, 1.0)
    cols_start(2, cols_of())
    rows_of(A, 3, None, False)
    rows_start(3)
    v = cols_done(2)
    rows_of(E, 2, v, True)
    rows_start(2)
    for b in range(BLOCKS):
        s_t[:, b * 128:(b + 1) * 128] = s_bf[b * 128:(b + 1) * 128, :].T
    z_wide = part
    rows_done(3, z_wide, factor)

    def probs(b, carry):
        rows = pl.ds(pl.multiple_of(b * 128, 128), 128)
        w = z_wide[rows, :]
        for k in range(TILE_COLS // 128):
            A[rows, k * 128:(k + 1) * 128] = A[rows, k * 128:(k + 1) * 128] * w
        return carry

    lax.fori_loop(0, BLOCKS, probs, 0)
    rows_done(2, u_wide, factor)

    def quarter(q):
        lo = q * QUARTER

        def one(b, carry):
            rows = pl.ds(pl.multiple_of(b * 128, 128), 128)
            u = u_wide[rows, :]
            for k in range(QUARTER // 128):
                at = slice(lo + k * 128, lo + (k + 1) * 128)
                L[rows, at] = (A[rows, at] - E[rows, at] * u).astype(BF16)
            return carry

        lax.fori_loop(0, BLOCKS, one, 0)
        cols = slice(lo, lo + QUARTER)
        g = jnp.dot(s_t[...], L[:, cols], preferred_element_type=F32)
        inv = sw_inv[:, cols]
        inner = jnp.sum(sw_bf[:, cols].astype(F32) * g, axis=0, keepdims=True)
        g = (g - sw_raw[:, cols].astype(F32) * (inv * inner)) * inv
        G[q] = g.reshape(NY, NZ, 8, QUARTER)

    def steps(q, way):
        return NZ // 2 if (q < 2) == (way == 1) else NZ // 2 - 1

    def ring(q, k, way):
        buf, send, recv = (ring_r, rr_send, rr_recv) if way == 1 else (ring_l, rl_send, rl_recv)
        if k >= steps(q, way):
            return
        dest = (z + way * (steps(q, way) - k) + NZ) % NZ
        if k == 0:
            src = G.at[q, :, dest]
        else:
            wait_bytes(buf.at[q, k - 1], recv.at[q, k - 1])
            buf[q, k - 1] = buf[q, k - 1] + G[q, :, dest]
            src = buf.at[q, k - 1]
        remote(src, buf.at[q, k], send.at[q, k], recv.at[q, k], dev(0, way, 0, 0)).start()

    def turned_rows(core_of, x_of, count):
        return pl.ds(pl.multiple_of((core_of * NX + x_of) * 32, 32), 32 * count)

    def h_block(b):
        rows = slice(b * ROWS, (b + 1) * ROWS)
        A[rows, 0:D] = jnp.dot(L[rows, :], sw_t[...], preferred_element_type=F32)

    def h_finish():
        def one(b, carry):
            rows = pl.ds(pl.multiple_of(b * 128, 128), 128)
            h = A[rows, 0:D]
            inner = jnp.sum(s_bf[rows, :].astype(F32) * h, axis=1, keepdims=True)
            inv = jnp.concatenate([s_inv[rows, :]] * 2, axis=1)
            h = (h - s_raw[rows, :].astype(F32) * inv * inner) * inv
            turned = h.T
            for p in range(NX * NC):
                E[turned_rows(p % NC, p // NC, 1), rows] = turned[p * 32:(p + 1) * 32, :]
            return carry

        lax.fori_loop(0, BLOCKS, one, 0)

    core = remote(E.at[turned_rows(1 - c, 0, NX), 0:TILE_ROWS], h_core, hc_send, hc_recv, dev(0, 0, 0, 1))

    def h_spread():
        core.wait_recv()

        def add(i, carry):
            here = turned_rows(c, i, 1)
            E[here, 0:TILE_ROWS] = E[here, 0:TILE_ROWS] + h_core[pl.ds(pl.multiple_of(i * 32, 32), 32), :]
            return carry

        lax.fori_loop(0, NX, add, 0)
        for i, (dy, dx) in enumerate(sheet):
            to_y, to_x = (y + dy) % NY, (x + dx) % NX
            remote(
                E.at[turned_rows(c, to_x, 1), block_rows(to_y)], h_in.at[i], h_send, h_recv, dev(dy, 0, dx, 0)
            ).start()

    def h_done():
        wait_bytes(h_in, h_recv)
        total = E[turned_rows(c, x, 1), block_rows(y)]
        for i in range(len(sheet)):
            total = total + h_in[i]
        hout_ref[...] = total

    between = [
        lambda: (h_block(0), h_block(1)), lambda: (h_block(2), h_block(3)), lambda: (h_finish(), core.start()),
        lambda: None, h_spread,
    ]

    for q in range(4):
        quarter(q)
        ring(q, 0, 1)
        ring(q, 0, -1)
    for k in range(1, NZ // 2):
        for q in range(4):
            ring(q, k, 1)
            ring(q, k, -1)
            if between:
                between.pop(0)()

    for q in range(4):
        last_r, last_l = steps(q, 1) - 1, steps(q, -1) - 1
        wait_bytes(ring_r.at[q, last_r], rr_recv.at[q, last_r])
        wait_bytes(ring_l.at[q, last_l], rl_recv.at[q, last_l])
        g_sum[q] = G[q, :, z] + ring_r[q, last_r] + ring_l[q, last_l]
        for o in (2, 1, 3):
            remote(
                g_sum.at[q, (y + o) % NY], g_out.at[q, o - 1], a_send.at[q], a_recv.at[q], dev(o, 0, 0, 0)
            ).start()
        wout_ref[:, pl.ds(pl.multiple_of(y * TILE_COLS + q * QUARTER, QUARTER), QUARTER)] = g_sum[q, y]
    h_done()
    for q in range(4):
        wait_bytes(g_out.at[q], a_recv.at[q])
        for o in range(1, NY):
            at = pl.multiple_of(((y + NY - o) % NY) * TILE_COLS + q * QUARTER, QUARTER)
            wout_ref[:, pl.ds(at, QUARTER)] = g_out[q, o - 1]

    for buf, send, fsend in ((t_in, t_send, t_fsend), (s_in, s_send, s_fsend)):
        wait_bytes(buf.at[:, 0], send)
        wait_bytes(buf.at[:, 0], fsend)
    for r in range(BALANCE_STEPS):
        wait_bytes(c_in.at[r], c_send.at[r])
    for r in range(BALANCE_STEPS + 1):
        wait_bytes(r_in.at[r], r_send.at[r])
    for q in range(4):
        for k in range(steps(q, 1)):
            wait_bytes(ring_r.at[q, k], rr_send.at[q, k])
        for k in range(steps(q, -1)):
            wait_bytes(ring_l.at[q, k], rl_send.at[q, k])
        wait_bytes(g_out.at[q], a_send.at[q])
    core.wait_send()
    wait_bytes(h_in, h_send)


def shards(student_features, teacher_features, student_weight, teacher_weight):
    crops_all = student_features.shape[0] * lax.axis_size("crop")
    factor = LOSS_SCALE / (STUDENT_TEMP * crops_all)
    vmem = pl.BlockSpec(memory_space=pltpu.VMEM)
    hbm = pl.BlockSpec(memory_space=pl.ANY)
    peers, sheet = NY * NX * NC - 1, NY * NX - 1
    v = pltpu.VMEM
    dma = pltpu.SemaphoreType.DMA
    scratch = [
        v((TILE_ROWS, TILE_COLS), F32), v((TILE_ROWS, TILE_COLS), F32),
        v((D, TILE_COLS), BF16), v((D, TILE_COLS), BF16),
        v((D, TILE_COLS), BF16), v((D, TILE_COLS), BF16),
        v((TILE_COLS, D), BF16), v((1, TILE_COLS), F32),
        v((TILE_ROWS, D), BF16), v((TILE_ROWS, D), BF16), v((D, TILE_ROWS), BF16),
        v((TILE_ROWS, D), BF16), v((TILE_ROWS, 128), F32),
        v((TILE_ROWS, 128), F32), v((TILE_ROWS, 128), F32),
        v((2, 2, PIECE, D), F32), v((2, 2, PIECE, D), F32),
        v((NY - 1, 2, 2, PIECE, D), F32), v((NY - 1, 2, 2, PIECE, D), F32),
        v((BALANCE_STEPS, 1, TILE_COLS), F32), v((BALANCE_STEPS, NZ - 1, 1, TILE_COLS), F32),
        v((BALANCE_STEPS + 1, BLOCKS, 128), F32), v((BALANCE_STEPS + 1, peers, BLOCKS, 128), F32),
        v((16, 128), F32), v((8, TILE_COLS), F32),
        v((TILE_ROWS, TILE_COLS), BF16),
        v((4, NY, NZ, 8, QUARTER), F32),
        v((4, NZ // 2, NY, 8, QUARTER), F32), v((4, NZ // 2, NY, 8, QUARTER), F32),
        v((4, NY, 8, QUARTER), F32), v((4, NY - 1, 8, QUARTER), F32),
        v((NX * 32, TILE_ROWS), F32), v((sheet, 32, ROWS), F32),
        dma((2,)),
        dma, dma((3, 2)), dma, dma((3, 2)),
        dma, dma((3, 2)), dma, dma((3, 2)),
        dma((3,)), dma((3,)), dma((4,)), dma((4,)),
        dma((4, 4)), dma((4, 4)), dma((4, 4)), dma((4, 4)),
        dma((4,)), dma((4,)), dma, dma, dma, dma,
    ]
    weight_grad, turned = pl.pallas_call(
        functools.partial(kernel, factor),
        out_shape=(
            jax.ShapeDtypeStruct((D // (NY * NZ), NY * TILE_COLS), F32),
            jax.ShapeDtypeStruct((D // (NX * NC), ROWS), F32),
        ),
        in_specs=[vmem, vmem, hbm, hbm],
        out_specs=(vmem, vmem),
        scratch_shapes=scratch,
        compiler_params=pltpu.CompilerParams(
            collective_id=0, has_side_effects=True, vmem_limit_bytes=53 * 1024 * 1024
        ),
        name="prototype_head",
    )(teacher_features, student_features, teacher_weight, student_weight)
    def hand_over(a_ref, b_ref, a_out, b_out):
        a_out[...] = a_ref[...]
        b_out[...] = b_ref[...]

    weight_grad, turned = pl.pallas_call(
        hand_over,
        out_shape=(
            jax.ShapeDtypeStruct(weight_grad.shape, F32),
            jax.ShapeDtypeStruct(turned.shape, F32),
        ),
        in_specs=[vmem, vmem],
        out_specs=(vmem, vmem),
        name="hand_over",
    )(weight_grad, turned)
    return weight_grad, turned.T


def solution(mesh):
    return jax.shard_map(
        shards,
        mesh=mesh,
        in_specs=(P("crop", None), P("crop", None), P(None, "proto"), P(None, "proto")),
        out_specs=(P("crop", "proto"), P("crop", "proto")),
        check_vma=False,
    )
```

```python
import functools
import math

import jax
import jax.numpy as jnp
from jax import lax
from jax.experimental import pallas as pl
from jax.experimental.pallas import tpu as pltpu
from jax.sharding import PartitionSpec as P

BALANCE_STEPS = 3
LOSS_SCALE = 4194304
EPSILON = 1e-06
TEACHER_TEMP = 0.07
STUDENT_TEMP = 0.1
LOG2E = math.log2(math.e)

NY, NZ, NX, NC = 4, 8, 4, 2
D = 256
ROWS = 384
TILE_ROWS = NY * ROWS
TILE_COLS = 2048
HALF = TILE_COLS // 2
QUARTER = TILE_COLS // 4
BLOCKS = TILE_ROWS // 128
PIECE = ROWS // 4
MESH = pl.DeviceIdType.MESH
F32, BF16 = jnp.float32, jnp.bfloat16


def kernel(
    factor,
    t_ref, s_ref, tw_hbm, sw_hbm,
    wout_ref, hout_ref,
    E, A, tw_raw, sw_raw, tw_bf, sw_bf, sw_t, sw_inv, t_bf, s_bf, s_t, s_raw, s_inv,
    u_wide, part, t_src, s_src, t_in, s_in,
    y_own, y_src, y_in, c_src, c_in, r_src, r_in, flat_ref,
    L, G, ring_r, ring_l, g_sum, g_out, h_core, h_in,
    load_sem, y_send, y_recv, t_send, t_recv, t_fsend, t_frecv, s_send, s_recv, s_fsend, s_frecv,
    c_send, c_recv, r_send, r_recv,
    rr_send, rr_recv, rl_send, rl_recv, a_send, a_recv, hc_send, hc_recv, h_send, h_recv,
):
    crop, proto = lax.axis_index("crop"), lax.axis_index("proto")
    y, z, x, c = crop // NZ, crop % NZ, proto // NC, proto % NC

    def dev(dy, dz, dx, dc):
        return (((y + dy) % NY) * NZ + (z + dz) % NZ, ((x + dx) % NX) * NC + (c + dc) % NC)

    def remote(src, dst, send, recv, to):
        return pltpu.make_async_remote_copy(
            src_ref=src, dst_ref=dst, send_sem=send, recv_sem=recv, device_id=to, device_id_type=MESH
        )

    def wait_bytes(buf, sem):
        pltpu.make_async_copy(buf, buf, sem).wait()

    def far(d, n):
        return min(d, n - d)

    plane = sorted(
        ((dy, dx, dc) for dy in range(NY) for dx in range(NX) for dc in range(NC) if (dy, dx, dc) != (0, 0, 0)),
        key=lambda o: -(far(o[0], NY) + far(o[1], NX)),
    )
    sheet = sorted(
        ((dy, dx) for dy in range(NY) for dx in range(NX) if (dy, dx) != (0, 0)),
        key=lambda o: -(far(o[0], NY) + far(o[1], NX)),
    )
    line = sorted(range(1, NZ), key=lambda d: -far(d, NZ))

    barrier = pltpu.get_barrier_semaphore()
    for dy, dx, dc in plane:
        pl.semaphore_signal(barrier, inc=1, device_id=dev(dy, 0, dx, dc), device_id_type=MESH)
    for dz in line:
        pl.semaphore_signal(barrier, inc=1, device_id=dev(0, dz, 0, 0), device_id_type=MESH)

    col0 = pl.multiple_of(y * TILE_COLS, TILE_COLS)
    load_t = pltpu.make_async_copy(tw_hbm.at[:, pl.ds(col0, TILE_COLS)], tw_raw, load_sem.at[0])
    load_s = pltpu.make_async_copy(sw_hbm.at[:, pl.ds(col0, TILE_COLS)], sw_raw, load_sem.at[1])
    load_t.start()
    loads = {}
    for o in (2, 1, 3):
        col = pl.multiple_of(((y + o) % NY) * TILE_COLS, TILE_COLS)
        loads[o] = pltpu.make_async_copy(
            tw_hbm.at[:, pl.ds(col, TILE_COLS)], L.at[(o - 1) * D:o * D, :], load_sem.at[1 + o]
        )
        loads[o].start()
    load_s.start()

    def block_rows(block):
        return pl.ds(pl.multiple_of(block * ROWS, ROWS), ROWS)

    def normalise(raw, out, inv_ref):
        def one(q, carry):
            cols = pl.ds(pl.multiple_of(q * QUARTER, QUARTER), QUARTER)
            w = raw[:, cols].astype(F32)
            inv = 1.0 / jnp.sqrt(jnp.sum(w * w, axis=0, keepdims=True) + EPSILON)
            out[:, cols] = (w * inv).astype(BF16)
            if inv_ref is not None:
                inv_ref[:, cols] = inv
            return carry

        lax.fori_loop(0, 4, one, 0)

    t32 = t_ref[...].astype(F32)
    t_own = (t32 * (1.0 / jnp.sqrt(jnp.sum(t32 * t32, axis=1, keepdims=True) + EPSILON))).astype(BF16)
    t_bf[block_rows(y), :] = t_own
    t_src[...] = t_own.astype(F32).reshape(2, 2, PIECE, D)
    s_src[...] = s_ref[...].astype(F32).reshape(2, 2, PIECE, D)

    pl.semaphore_wait(barrier, len(plane) + NZ - 1)

    def gather_start(src, dst, send, recv):
        for piece, way in ((0, 1), (1, 3), (1, 1), (0, 3)):
            remote(src.at[c, piece], dst.at[way - 1, c, piece], send, recv.at[way - 1, piece], dev(way, 0, 0, 0)).start()

    def gather_relay(dst, send, recv):
        for piece, way in ((0, 1), (1, 3)):
            wait_bytes(dst.at[way - 1, c, piece], recv.at[way - 1, piece])
            remote(
                dst.at[way - 1, c, piece], dst.at[1, c, piece], send, recv.at[1, piece], dev(way, 0, 0, 0)
            ).start()

    def gather_core(dst, fsend, frecv, way, piece):
        remote(
            dst.at[way - 1, c, piece], dst.at[way - 1, c, piece], fsend, frecv.at[way - 1, piece], dev(0, 0, 0, 1)
        ).start()

    def gather_near(dst, recv, fsend, frecv):
        gather_core(dst, fsend, frecv, 1, 0)
        gather_core(dst, fsend, frecv, 3, 1)
        for piece, way in ((1, 1), (0, 3)):
            wait_bytes(dst.at[way - 1, c, piece], recv.at[way - 1, piece])
            gather_core(dst, fsend, frecv, way, piece)

    def gather_far(dst, recv, fsend, frecv):
        for piece in range(2):
            wait_bytes(dst.at[1, c, piece], recv.at[1, piece])
            gather_core(dst, fsend, frecv, 2, piece)

    def gather_done(dst, frecv, way):
        for piece in range(2):
            wait_bytes(dst.at[way - 1, 1 - c, piece], frecv.at[way - 1, piece])
        return (y + NY - way) % NY, dst[way - 1].reshape(ROWS, D)

    def cols_start(r, half, sums):
        c_src[r, half] = jnp.sum(sums, axis=0, keepdims=True)
        for i, dz in enumerate(line):
            remote(
                c_src.at[r, half], c_in.at[r, half, i], c_send.at[r, half], c_recv.at[r, half], dev(0, dz, 0, 0)
            ).start()

    def cols_done(r, half):
        wait_bytes(c_in.at[r, half], c_recv.at[r, half])
        total = c_src[r, half]
        for i in range(len(line)):
            total = total + c_in[r, half, i]
        return 1.0 / total

    gather_start(t_src, t_in, t_send, t_recv)
    load_t.wait()
    normalise(tw_raw, tw_bf, None)

    def teacher_exp(rows, weight, cols):
        return jnp.exp2(jnp.dot(t_bf[rows, :], weight[:, cols], preferred_element_type=F32) * (LOG2E / TEACHER_TEMP))

    def halves(one):
        def step(half, carry):
            one(pl.ds(pl.multiple_of(half * HALF, HALF), HALF))
            return carry

        lax.fori_loop(0, 2, step, 0)

    def exp_block(block):
        rows = block_rows(block)

        def one(cols):
            E[rows, cols] = teacher_exp(rows, tw_bf, cols)

        halves(one)

    def own_sums(weight, dst, keep):
        rows = block_rows(y)

        def one(cols):
            e = teacher_exp(rows, weight, cols)
            if keep:
                E[rows, cols] = e
            sums = jnp.sum(e.reshape(ROWS // 8, 8, HALF), axis=0)
            dst[:, cols] = jnp.sum(sums, axis=0, keepdims=True)

        halves(one)

    def sums_for(o):
        loads[o].wait()
        weight = L.at[(NY + o - 2) * D:(NY + o - 1) * D, :]
        normalise(L.at[(o - 1) * D:o * D, :], weight, None)
        own_sums(weight, y_src.at[o - 1], False)
        remote(y_src.at[o - 1], y_in.at[o - 1], y_send, y_recv.at[o - 1], dev(o, 0, 0, 0)).start()

    own_sums(tw_bf, y_own, True)
    sums_for(2)
    sums_for(1)
    gather_relay(t_in, t_send, t_recv)
    sums_for(3)
    gather_near(t_in, t_recv, t_fsend, t_frecv)
    for o in range(1, NY):
        wait_bytes(y_in.at[o - 1], y_recv.at[o - 1])
    col_sums = y_own[...] + y_in[0] + y_in[1] + y_in[2]
    cols_start(0, 0, col_sums[:, :HALF])
    cols_start(0, 1, col_sums[:, HALF:])
    for way in (1, 3, 2):
        if way == 3:
            gather_far(t_in, t_recv, t_fsend, t_frecv)
        block, rows = gather_done(t_in, t_frecv, way)
        t_bf[block_rows(block), :] = rows.astype(BF16)
        exp_block(block)
    gather_start(s_src, s_in, s_send, s_recv)

    lane = lax.broadcasted_iota(jnp.int32, (8, 128), 1)
    sublane = lax.broadcasted_iota(jnp.int32, (8, 128), 0)

    def rows_of(src, r, scaled, store):
        for half in range(2):
            scale = cols_done(r, half) if scaled else None

            def one(b, carry):
                rows = pl.ds(pl.multiple_of(b * 128, 128), 128)
                acc = part[rows, :] if half else None
                for k in range(HALF // 128):
                    cols = slice(half * HALF + k * 128, half * HALF + (k + 1) * 128)
                    term = src[rows, cols]
                    if scaled:
                        term = term * scale[:, k * 128:(k + 1) * 128]
                    if store:
                        src[rows, cols] = term
                    acc = term if acc is None else acc + term
                part[rows, :] = acc
                return carry

            lax.fori_loop(0, BLOCKS, one, 0)

        def packed(g0, g1):
            out = None
            for base in range(g0, g1, 16):
                some = jnp.zeros((8, 128), F32)
                for g in range(base, base + 16):
                    total = jnp.sum(part[8 * g:8 * g + 8, :], axis=1, keepdims=True)
                    some = jnp.where(lane == g - g0, total, some)
                out = some if out is None else out + some
            return out

        r_src[r, 0:8, :] = packed(0, 128)
        rest = packed(128, 192)
        rest = rest + pltpu.roll(pltpu.roll(rest, 64, 1), 4, 0)
        r_src[r, 8:12, :] = rest[0:4, :]

    def rows_start(r):
        for i, (dy, dx, dc) in enumerate(plane):
            remote(r_src.at[r], r_in.at[r, i], r_send.at[r], r_recv.at[r], dev(dy, 0, dx, dc)).start()

    def rows_done(r, dst, scale):
        wait_bytes(r_in.at[r], r_recv.at[r])
        total = r_src[r]
        for i in range(len(plane)):
            total = total + r_in[r, i]
        flat_ref[0:BLOCKS, :] = scale / total
        low, rest = flat_ref[0:8, :], flat_ref[8:16, :]
        high = jnp.where(sublane < 4, rest, pltpu.roll(pltpu.roll(rest, 64, 1), 4, 0))
        for g in range(TILE_ROWS // 8):
            value = low[:, g:g + 1] if g < 128 else high[:, g - 128:g - 127]
            dst[8 * g:8 * g + 8, :] = jnp.broadcast_to(value, (8, 128))

    def cols_of(r):
        for half in range(2):

            def one(b, acc):
                rows = pl.ds(pl.multiple_of(b * 128, 128), 128)
                u = u_wide[rows, :]
                out = []
                for k in range(HALF // 128):
                    e = E[rows, half * HALF + k * 128:half * HALF + (k + 1) * 128] * u
                    out.append(acc[k] + jnp.sum(e.reshape(16, 8, 128), axis=0))
                return tuple(out)

            zero = tuple(jnp.zeros((8, 128), F32) for _ in range(HALF // 128))
            cols_start(r, half, jnp.concatenate(lax.fori_loop(0, BLOCKS, one, zero), axis=1))

    def student_exp():
        def one(i, carry):
            rows = pl.ds(pl.multiple_of((i // 2) * ROWS, ROWS), ROWS)
            cols = pl.ds(pl.multiple_of((i % 2) * HALF, HALF), HALF)
            A[rows, cols] = jnp.exp2(
                jnp.dot(s_bf[rows, :], sw_bf[:, cols], preferred_element_type=F32) * (LOG2E / STUDENT_TEMP)
            )
            return carry

        lax.fori_loop(0, 2 * NY, one, 0)

    def student_block(block, raw):
        inv = 1.0 / jnp.sqrt(jnp.sum(raw * raw, axis=1, keepdims=True) + EPSILON)
        unit = raw * inv
        rows = block_rows(block)
        s_raw[rows, :] = raw.astype(BF16)
        s_inv[rows, :] = jnp.broadcast_to(inv, (ROWS, 128))
        s_bf[rows, :] = unit.astype(BF16)

    rows_of(E, 0, True, False)
    rows_start(0)
    load_s.wait()
    normalise(sw_raw, sw_bf, sw_inv)
    for q in range(4):
        sw_t[q * QUARTER:(q + 1) * QUARTER, :] = sw_bf[:, q * QUARTER:(q + 1) * QUARTER].T
    student_block(y, s_src[...].reshape(ROWS, D))
    gather_relay(s_in, s_send, s_recv)
    rows_done(0, u_wide, 1.0)
    cols_of(1)
    gather_near(s_in, s_recv, s_fsend, s_frecv)
    gather_far(s_in, s_recv, s_fsend, s_frecv)
    for way in (1, 3, 2):
        student_block(*gather_done(s_in, s_frecv, way))
    rows_of(E, 1, True, False)
    rows_start(1)
    student_exp()
    rows_done(1, u_wide, 1.0)
    cols_of(2)
    rows_of(A, 3, False, False)
    rows_start(3)
    rows_of(E, 2, True, True)
    rows_start(2)
    for b in range(BLOCKS):
        s_t[:, b * 128:(b + 1) * 128] = s_bf[b * 128:(b + 1) * 128, :].T
    z_wide = part
    rows_done(3, z_wide, factor)

    def probs(b, carry):
        rows = pl.ds(pl.multiple_of(b * 128, 128), 128)
        w = z_wide[rows, :]
        for k in range(TILE_COLS // 128):
            A[rows, k * 128:(k + 1) * 128] = A[rows, k * 128:(k + 1) * 128] * w
        return carry

    lax.fori_loop(0, BLOCKS, probs, 0)
    rows_done(2, u_wide, factor)

    def quarter(q):
        lo = q * QUARTER

        def one(b, carry):
            rows = pl.ds(pl.multiple_of(b * 128, 128), 128)
            u = u_wide[rows, :]
            for k in range(QUARTER // 128):
                at = slice(lo + k * 128, lo + (k + 1) * 128)
                L[rows, at] = (A[rows, at] - E[rows, at] * u).astype(BF16)
            return carry

        lax.fori_loop(0, BLOCKS, one, 0)
        cols = slice(lo, lo + QUARTER)
        g = jnp.dot(s_t[...], L[:, cols], preferred_element_type=F32)
        inv = sw_inv[:, cols]
        inner = jnp.sum(sw_bf[:, cols].astype(F32) * g, axis=0, keepdims=True)
        g = (g - sw_raw[:, cols].astype(F32) * (inv * inner)) * inv
        G[q] = g.reshape(NY, NZ, 8, QUARTER)

    def steps(q, way):
        return NZ // 2 if (q < 2) == (way == 1) else NZ // 2 - 1

    def ring(q, k, way):
        buf, send, recv = (ring_r, rr_send, rr_recv) if way == 1 else (ring_l, rl_send, rl_recv)
        if k >= steps(q, way):
            return
        dest = (z + way * (steps(q, way) - k) + NZ) % NZ
        if k == 0:
            src = G.at[q, :, dest]
        else:
            wait_bytes(buf.at[q, k - 1], recv.at[q, k - 1])
            buf[q, k - 1] = buf[q, k - 1] + G[q, :, dest]
            src = buf.at[q, k - 1]
        remote(src, buf.at[q, k], send.at[q, k], recv.at[q, k], dev(0, way, 0, 0)).start()

    def turned_rows(core_of, x_of, count):
        return pl.ds(pl.multiple_of((core_of * NX + x_of) * 32, 32), 32 * count)

    def h_block(b):
        rows = slice(b * ROWS, (b + 1) * ROWS)
        A[rows, 0:D] = jnp.dot(L[rows, :], sw_t[...], preferred_element_type=F32)

    def h_finish():
        def one(b, carry):
            rows = pl.ds(pl.multiple_of(b * 128, 128), 128)
            h = A[rows, 0:D]
            inner = jnp.sum(s_bf[rows, :].astype(F32) * h, axis=1, keepdims=True)
            inv = jnp.concatenate([s_inv[rows, :]] * 2, axis=1)
            h = (h - s_raw[rows, :].astype(F32) * inv * inner) * inv
            turned = h.T
            for p in range(NX * NC):
                E[turned_rows(p % NC, p // NC, 1), rows] = turned[p * 32:(p + 1) * 32, :]
            return carry

        lax.fori_loop(0, BLOCKS, one, 0)

    core = remote(E.at[turned_rows(1 - c, 0, NX), 0:TILE_ROWS], h_core, hc_send, hc_recv, dev(0, 0, 0, 1))

    def h_spread():
        core.wait_recv()

        def add(i, carry):
            here = turned_rows(c, i, 1)
            E[here, 0:TILE_ROWS] = E[here, 0:TILE_ROWS] + h_core[pl.ds(pl.multiple_of(i * 32, 32), 32), :]
            return carry

        lax.fori_loop(0, NX, add, 0)
        for i, (dy, dx) in enumerate(sheet):
            to_y, to_x = (y + dy) % NY, (x + dx) % NX
            remote(
                E.at[turned_rows(c, to_x, 1), block_rows(to_y)], h_in.at[i], h_send, h_recv, dev(dy, 0, dx, 0)
            ).start()

    def h_done():
        wait_bytes(h_in, h_recv)
        total = E[turned_rows(c, x, 1), block_rows(y)]
        for i in range(len(sheet)):
            total = total + h_in[i]
        hout_ref[...] = total

    between = [
        lambda: (h_block(0), h_block(1)), lambda: (h_block(2), h_block(3)), lambda: (h_finish(), core.start()),
        lambda: None, h_spread,
    ]

    for q in range(4):
        quarter(q)
        ring(q, 0, 1)
        ring(q, 0, -1)
    for k in range(1, NZ // 2):
        for q in range(4):
            ring(q, k, 1)
            ring(q, k, -1)
            if between:
                between.pop(0)()

    for q in range(4):
        last_r, last_l = steps(q, 1) - 1, steps(q, -1) - 1
        wait_bytes(ring_r.at[q, last_r], rr_recv.at[q, last_r])
        wait_bytes(ring_l.at[q, last_l], rl_recv.at[q, last_l])
        g_sum[q] = G[q, :, z] + ring_r[q, last_r] + ring_l[q, last_l]
        for o in (2, 1, 3):
            remote(
                g_sum.at[q, (y + o) % NY], g_out.at[q, o - 1], a_send.at[q], a_recv.at[q], dev(o, 0, 0, 0)
            ).start()
        wout_ref[:, pl.ds(pl.multiple_of(y * TILE_COLS + q * QUARTER, QUARTER), QUARTER)] = g_sum[q, y]
    h_done()
    for q in range(4):
        wait_bytes(g_out.at[q], a_recv.at[q])
        for o in range(1, NY):
            at = pl.multiple_of(((y + NY - o) % NY) * TILE_COLS + q * QUARTER, QUARTER)
            wout_ref[:, pl.ds(at, QUARTER)] = g_out[q, o - 1]

    for buf, send, fsend in ((t_in, t_send, t_fsend), (s_in, s_send, s_fsend)):
        wait_bytes(buf.at[:, 0], send)
        wait_bytes(buf.at[:, 0], fsend)
    wait_bytes(y_in, y_send)
    for r in range(BALANCE_STEPS):
        for half in range(2):
            wait_bytes(c_in.at[r, half], c_send.at[r, half])
    for r in range(BALANCE_STEPS + 1):
        wait_bytes(r_in.at[r], r_send.at[r])
    for q in range(4):
        for k in range(steps(q, 1)):
            wait_bytes(ring_r.at[q, k], rr_send.at[q, k])
        for k in range(steps(q, -1)):
            wait_bytes(ring_l.at[q, k], rl_send.at[q, k])
        wait_bytes(g_out.at[q], a_send.at[q])
    core.wait_send()
    wait_bytes(h_in, h_send)


def shards(student_features, teacher_features, student_weight, teacher_weight):
    crops_all = student_features.shape[0] * lax.axis_size("crop")
    factor = LOSS_SCALE / (STUDENT_TEMP * crops_all)
    vmem = pl.BlockSpec(memory_space=pltpu.VMEM)
    hbm = pl.BlockSpec(memory_space=pl.ANY)
    peers, sheet = NY * NX * NC - 1, NY * NX - 1
    v = pltpu.VMEM
    dma = pltpu.SemaphoreType.DMA
    scratch = [
        v((TILE_ROWS, TILE_COLS), F32), v((TILE_ROWS, TILE_COLS), F32),
        v((D, TILE_COLS), BF16), v((D, TILE_COLS), BF16),
        v((D, TILE_COLS), BF16), v((D, TILE_COLS), BF16),
        v((TILE_COLS, D), BF16), v((1, TILE_COLS), F32),
        v((TILE_ROWS, D), BF16), v((TILE_ROWS, D), BF16), v((D, TILE_ROWS), BF16),
        v((TILE_ROWS, D), BF16), v((TILE_ROWS, 128), F32),
        v((TILE_ROWS, 128), F32), v((TILE_ROWS, 128), F32),
        v((2, 2, PIECE, D), F32), v((2, 2, PIECE, D), F32),
        v((NY - 1, 2, 2, PIECE, D), F32), v((NY - 1, 2, 2, PIECE, D), F32),
        v((1, TILE_COLS), F32), v((NY - 1, 1, TILE_COLS), F32), v((NY - 1, 1, TILE_COLS), F32),
        v((BALANCE_STEPS, 2, 1, HALF), F32), v((BALANCE_STEPS, 2, NZ - 1, 1, HALF), F32),
        v((BALANCE_STEPS + 1, BLOCKS, 128), F32), v((BALANCE_STEPS + 1, peers, BLOCKS, 128), F32),
        v((16, 128), F32),
        v((TILE_ROWS, TILE_COLS), BF16),
        v((4, NY, NZ, 8, QUARTER), F32),
        v((4, NZ // 2, NY, 8, QUARTER), F32), v((4, NZ // 2, NY, 8, QUARTER), F32),
        v((4, NY, 8, QUARTER), F32), v((4, NY - 1, 8, QUARTER), F32),
        v((NX * 32, TILE_ROWS), F32), v((sheet, 32, ROWS), F32),
        dma((5,)), dma, dma((3,)),
        dma, dma((3, 2)), dma, dma((3, 2)),
        dma, dma((3, 2)), dma, dma((3, 2)),
        dma((3, 2)), dma((3, 2)), dma((4,)), dma((4,)),
        dma((4, 4)), dma((4, 4)), dma((4, 4)), dma((4, 4)),
        dma((4,)), dma((4,)), dma, dma, dma, dma,
    ]
    weight_grad, turned = pl.pallas_call(
        functools.partial(kernel, factor),
        out_shape=(
            jax.ShapeDtypeStruct((D // (NY * NZ), NY * TILE_COLS), F32),
            jax.ShapeDtypeStruct((D // (NX * NC), ROWS), F32),
        ),
        in_specs=[vmem, vmem, hbm, hbm],
        out_specs=(vmem, vmem),
        scratch_shapes=scratch,
        compiler_params=pltpu.CompilerParams(
            collective_id=0, has_side_effects=True, vmem_limit_bytes=53 * 1024 * 1024
        ),
        name="prototype_head",
    )(teacher_features, student_features, teacher_weight, student_weight)
    return weight_grad, turned.T


def solution(mesh):
    return jax.shard_map(
        shards,
        mesh=mesh,
        in_specs=(P("crop", None), P("crop", None), P(None, "proto"), P(None, "proto")),
        out_specs=(P("crop", "proto"), P("crop", "proto")),
        check_vma=False,
    )
```

```python
import functools
import math

import jax
import jax.numpy as jnp
from jax import lax
from jax.experimental import pallas as pl
from jax.experimental.pallas import tpu as pltpu
from jax.sharding import PartitionSpec as P

BALANCE_STEPS = 3
LOSS_SCALE = 4194304
EPSILON = 1e-06
TEACHER_TEMP = 0.07
STUDENT_TEMP = 0.1
LOG2E = math.log2(math.e)

NY, NZ, NX, NC = 4, 8, 4, 2
D = 256
ROWS = 384
TILE_ROWS = NY * ROWS
TILE_COLS = 2048
HALF = TILE_COLS // 2
QUARTER = TILE_COLS // 4
BLOCKS = TILE_ROWS // 128
PIECE = ROWS // 4
MESH = pl.DeviceIdType.MESH
F32, BF16 = jnp.float32, jnp.bfloat16


def kernel(
    factor,
    t_ref, s_ref, tw_hbm, sw_hbm,
    wout_ref, hout_ref,
    E, A, tw_raw, sw_raw, tw_bf, sw_bf, sw_t, sw_inv, t_bf, s_bf, s_t, s_raw, s_inv,
    u_wide, part, t_src, s_src, t_in, s_in,
    y_own, y_src, y_in, c_src, c_in, r_src, r_in, flat_ref,
    L, G, ring_r, ring_l, g_sum, g_out, h_core, h_in,
    load_sem, y_send, y_recv, t_send, t_recv, t_fsend, t_frecv, s_send, s_recv, s_fsend, s_frecv,
    c_send, c_recv, r_send, r_recv,
    rr_send, rr_recv, rl_send, rl_recv, a_send, a_recv, hc_send, hc_recv, h_send, h_recv,
):
    crop, proto = lax.axis_index("crop"), lax.axis_index("proto")
    y, z, x, c = crop // NZ, crop % NZ, proto // NC, proto % NC

    def dev(dy, dz, dx, dc):
        return (((y + dy) % NY) * NZ + (z + dz) % NZ, ((x + dx) % NX) * NC + (c + dc) % NC)

    def remote(src, dst, send, recv, to):
        return pltpu.make_async_remote_copy(
            src_ref=src, dst_ref=dst, send_sem=send, recv_sem=recv, device_id=to, device_id_type=MESH
        )

    def wait_bytes(buf, sem):
        pltpu.make_async_copy(buf, buf, sem).wait()

    def far(d, n):
        return min(d, n - d)

    plane = sorted(
        ((dy, dx, dc) for dy in range(NY) for dx in range(NX) for dc in range(NC) if (dy, dx, dc) != (0, 0, 0)),
        key=lambda o: -(far(o[0], NY) + far(o[1], NX)),
    )
    sheet = sorted(
        ((dy, dx) for dy in range(NY) for dx in range(NX) if (dy, dx) != (0, 0)),
        key=lambda o: -(far(o[0], NY) + far(o[1], NX)),
    )
    line = sorted(range(1, NZ), key=lambda d: -far(d, NZ))

    barrier = pltpu.get_barrier_semaphore()
    for dy, dx, dc in plane:
        pl.semaphore_signal(barrier, inc=1, device_id=dev(dy, 0, dx, dc), device_id_type=MESH)
    for dz in line:
        pl.semaphore_signal(barrier, inc=1, device_id=dev(0, dz, 0, 0), device_id_type=MESH)

    col0 = pl.multiple_of(y * TILE_COLS, TILE_COLS)
    load_t = pltpu.make_async_copy(tw_hbm.at[:, pl.ds(col0, TILE_COLS)], tw_raw, load_sem.at[0])
    load_s = pltpu.make_async_copy(sw_hbm.at[:, pl.ds(col0, TILE_COLS)], sw_raw, load_sem.at[1])
    load_t.start()
    loads = {}
    for o in (2, 1, 3):
        col = pl.multiple_of(((y + o) % NY) * TILE_COLS, TILE_COLS)
        loads[o] = pltpu.make_async_copy(
            tw_hbm.at[:, pl.ds(col, TILE_COLS)], L.at[(o - 1) * D:o * D, :], load_sem.at[1 + o]
        )
        loads[o].start()
    load_s.start()

    def block_rows(block):
        return pl.ds(pl.multiple_of(block * ROWS, ROWS), ROWS)

    def normalise(raw, out, inv_ref):
        def one(q, carry):
            cols = pl.ds(pl.multiple_of(q * QUARTER, QUARTER), QUARTER)
            w = raw[:, cols].astype(F32)
            inv = 1.0 / jnp.sqrt(jnp.sum(w * w, axis=0, keepdims=True) + EPSILON)
            out[:, cols] = (w * inv).astype(BF16)
            if inv_ref is not None:
                inv_ref[:, cols] = inv
            return carry

        lax.fori_loop(0, 4, one, 0)

    t32 = t_ref[...].astype(F32)
    t_own = (t32 * (1.0 / jnp.sqrt(jnp.sum(t32 * t32, axis=1, keepdims=True) + EPSILON))).astype(BF16)
    t_bf[block_rows(y), :] = t_own
    t_src[...] = t_own.astype(F32).reshape(2, 2, PIECE, D)
    s_src[...] = s_ref[...].astype(F32).reshape(2, 2, PIECE, D)

    pl.semaphore_wait(barrier, len(plane) + NZ - 1)

    def gather_start(src, dst, send, recv):
        for piece, way in ((0, 1), (1, 3), (1, 1), (0, 3)):
            remote(src.at[c, piece], dst.at[way - 1, c, piece], send, recv.at[way - 1, piece], dev(way, 0, 0, 0)).start()

    def gather_relay(dst, send, recv):
        for piece, way in ((0, 1), (1, 3)):
            wait_bytes(dst.at[way - 1, c, piece], recv.at[way - 1, piece])
            remote(
                dst.at[way - 1, c, piece], dst.at[1, c, piece], send, recv.at[1, piece], dev(way, 0, 0, 0)
            ).start()

    def gather_core(dst, fsend, frecv, way, piece):
        remote(
            dst.at[way - 1, c, piece], dst.at[way - 1, c, piece], fsend, frecv.at[way - 1, piece], dev(0, 0, 0, 1)
        ).start()

    def gather_near(dst, recv, fsend, frecv):
        gather_core(dst, fsend, frecv, 1, 0)
        gather_core(dst, fsend, frecv, 3, 1)
        for piece, way in ((1, 1), (0, 3)):
            wait_bytes(dst.at[way - 1, c, piece], recv.at[way - 1, piece])
            gather_core(dst, fsend, frecv, way, piece)

    def gather_far(dst, recv, fsend, frecv):
        for piece in range(2):
            wait_bytes(dst.at[1, c, piece], recv.at[1, piece])
            gather_core(dst, fsend, frecv, 2, piece)

    def gather_done(dst, frecv, way):
        for piece in range(2):
            wait_bytes(dst.at[way - 1, 1 - c, piece], frecv.at[way - 1, piece])
        return (y + NY - way) % NY, dst[way - 1].reshape(ROWS, D)

    def cols_start(r, half, sums):
        c_src[r, half] = jnp.sum(sums, axis=0, keepdims=True)
        for i, dz in enumerate(line):
            remote(
                c_src.at[r, half], c_in.at[r, half, i], c_send.at[r, half], c_recv.at[r, half], dev(0, dz, 0, 0)
            ).start()

    def cols_done(r, half):
        wait_bytes(c_in.at[r, half], c_recv.at[r, half])
        total = c_src[r, half]
        for i in range(len(line)):
            total = total + c_in[r, half, i]
        return 1.0 / total

    gather_start(t_src, t_in, t_send, t_recv)
    load_t.wait()
    normalise(tw_raw, tw_bf, None)

    def teacher_exp(rows, weight, cols):
        return jnp.exp2(jnp.dot(t_bf[rows, :], weight[:, cols], preferred_element_type=F32) * (LOG2E / TEACHER_TEMP))

    def halves(one):
        def step(half, carry):
            one(pl.ds(pl.multiple_of(half * HALF, HALF), HALF))
            return carry

        lax.fori_loop(0, 2, step, 0)

    def exp_block(block):
        rows = block_rows(block)

        def one(cols):
            E[rows, cols] = teacher_exp(rows, tw_bf, cols)

        halves(one)

    def own_sums(weight, dst, keep):
        rows = block_rows(y)

        def one(cols):
            e = teacher_exp(rows, weight, cols)
            if keep:
                E[rows, cols] = e
            sums = jnp.sum(e.reshape(ROWS // 8, 8, HALF), axis=0)
            dst[:, cols] = jnp.sum(sums, axis=0, keepdims=True)

        halves(one)

    def sums_for(o):
        loads[o].wait()
        weight = L.at[(NY + o - 2) * D:(NY + o - 1) * D, :]
        normalise(L.at[(o - 1) * D:o * D, :], weight, None)
        own_sums(weight, y_src.at[o - 1], False)
        remote(y_src.at[o - 1], y_in.at[o - 1], y_send, y_recv.at[o - 1], dev(o, 0, 0, 0)).start()

    own_sums(tw_bf, y_own, True)
    sums_for(2)
    sums_for(1)
    sums_for(3)
    gather_relay(t_in, t_send, t_recv)
    gather_near(t_in, t_recv, t_fsend, t_frecv)
    for o in range(1, NY):
        wait_bytes(y_in.at[o - 1], y_recv.at[o - 1])
    col_sums = y_own[...] + y_in[0] + y_in[1] + y_in[2]
    cols_start(0, 0, col_sums[:, :HALF])
    cols_start(0, 1, col_sums[:, HALF:])
    for way in (1, 3, 2):
        if way == 3:
            gather_far(t_in, t_recv, t_fsend, t_frecv)
        block, rows = gather_done(t_in, t_frecv, way)
        t_bf[block_rows(block), :] = rows.astype(BF16)
        exp_block(block)
    gather_start(s_src, s_in, s_send, s_recv)

    lane = lax.broadcasted_iota(jnp.int32, (8, 128), 1)
    sublane = lax.broadcasted_iota(jnp.int32, (8, 128), 0)

    def rows_of(src, r, scaled, store):
        for half in range(2):
            scale = cols_done(r, half) if scaled else None

            def one(b, carry):
                rows = pl.ds(pl.multiple_of(b * 128, 128), 128)
                acc = part[rows, :] if half else None
                for k in range(HALF // 128):
                    cols = slice(half * HALF + k * 128, half * HALF + (k + 1) * 128)
                    term = src[rows, cols]
                    if scaled:
                        term = term * scale[:, k * 128:(k + 1) * 128]
                    if store:
                        src[rows, cols] = term
                    acc = term if acc is None else acc + term
                part[rows, :] = acc
                return carry

            lax.fori_loop(0, BLOCKS, one, 0)

        def packed(g0, g1):
            out = None
            for base in range(g0, g1, 16):
                some = jnp.zeros((8, 128), F32)
                for g in range(base, base + 16):
                    total = jnp.sum(part[8 * g:8 * g + 8, :], axis=1, keepdims=True)
                    some = jnp.where(lane == g - g0, total, some)
                out = some if out is None else out + some
            return out

        r_src[r, 0:8, :] = packed(0, 128)
        rest = packed(128, 192)
        rest = rest + pltpu.roll(pltpu.roll(rest, 64, 1), 4, 0)
        r_src[r, 8:12, :] = rest[0:4, :]

    def rows_start(r):
        for i, (dy, dx, dc) in enumerate(plane):
            remote(r_src.at[r], r_in.at[r, i], r_send.at[r], r_recv.at[r], dev(dy, 0, dx, dc)).start()

    def rows_done(r, dst, scale):
        wait_bytes(r_in.at[r], r_recv.at[r])
        total = r_src[r]
        for i in range(len(plane)):
            total = total + r_in[r, i]
        flat_ref[0:BLOCKS, :] = scale / total
        low, rest = flat_ref[0:8, :], flat_ref[8:16, :]
        high = jnp.where(sublane < 4, rest, pltpu.roll(pltpu.roll(rest, 64, 1), 4, 0))
        for g in range(TILE_ROWS // 8):
            value = low[:, g:g + 1] if g < 128 else high[:, g - 128:g - 127]
            dst[8 * g:8 * g + 8, :] = jnp.broadcast_to(value, (8, 128))

    def cols_of(r):
        for half in range(2):

            def one(b, acc):
                rows = pl.ds(pl.multiple_of(b * 128, 128), 128)
                u = u_wide[rows, :]
                out = []
                for k in range(HALF // 128):
                    e = E[rows, half * HALF + k * 128:half * HALF + (k + 1) * 128] * u
                    out.append(acc[k] + jnp.sum(e.reshape(16, 8, 128), axis=0))
                return tuple(out)

            zero = tuple(jnp.zeros((8, 128), F32) for _ in range(HALF // 128))
            cols_start(r, half, jnp.concatenate(lax.fori_loop(0, BLOCKS, one, zero), axis=1))

    def student_exp():
        def one(i, carry):
            rows = pl.ds(pl.multiple_of((i // 2) * ROWS, ROWS), ROWS)
            cols = pl.ds(pl.multiple_of((i % 2) * HALF, HALF), HALF)
            A[rows, cols] = jnp.exp2(
                jnp.dot(s_bf[rows, :], sw_bf[:, cols], preferred_element_type=F32) * (LOG2E / STUDENT_TEMP)
            )
            return carry

        lax.fori_loop(0, 2 * NY, one, 0)

    def student_block(block, raw):
        inv = 1.0 / jnp.sqrt(jnp.sum(raw * raw, axis=1, keepdims=True) + EPSILON)
        unit = raw * inv
        rows = block_rows(block)
        s_raw[rows, :] = raw.astype(BF16)
        s_inv[rows, :] = jnp.broadcast_to(inv, (ROWS, 128))
        s_bf[rows, :] = unit.astype(BF16)

    rows_of(E, 0, True, False)
    rows_start(0)
    load_s.wait()
    normalise(sw_raw, sw_bf, sw_inv)
    for q in range(4):
        sw_t[q * QUARTER:(q + 1) * QUARTER, :] = sw_bf[:, q * QUARTER:(q + 1) * QUARTER].T
    student_block(y, s_src[...].reshape(ROWS, D))
    gather_relay(s_in, s_send, s_recv)
    rows_done(0, u_wide, 1.0)
    cols_of(1)
    gather_near(s_in, s_recv, s_fsend, s_frecv)
    gather_far(s_in, s_recv, s_fsend, s_frecv)
    for way in (1, 3, 2):
        student_block(*gather_done(s_in, s_frecv, way))
    rows_of(E, 1, True, False)
    rows_start(1)
    student_exp()
    rows_done(1, u_wide, 1.0)
    cols_of(2)
    rows_of(A, 3, False, False)
    rows_start(3)
    rows_of(E, 2, True, True)
    rows_start(2)
    for b in range(BLOCKS):
        s_t[:, b * 128:(b + 1) * 128] = s_bf[b * 128:(b + 1) * 128, :].T
    z_wide = part
    rows_done(3, z_wide, factor)

    def probs(b, carry):
        rows = pl.ds(pl.multiple_of(b * 128, 128), 128)
        w = z_wide[rows, :]
        for k in range(TILE_COLS // 128):
            A[rows, k * 128:(k + 1) * 128] = A[rows, k * 128:(k + 1) * 128] * w
        return carry

    lax.fori_loop(0, BLOCKS, probs, 0)
    rows_done(2, u_wide, factor)

    def quarter(q):
        lo = q * QUARTER

        def one(b, carry):
            rows = pl.ds(pl.multiple_of(b * 128, 128), 128)
            u = u_wide[rows, :]
            for k in range(QUARTER // 128):
                at = slice(lo + k * 128, lo + (k + 1) * 128)
                L[rows, at] = (A[rows, at] - E[rows, at] * u).astype(BF16)
            return carry

        lax.fori_loop(0, BLOCKS, one, 0)
        cols = slice(lo, lo + QUARTER)
        g = jnp.dot(s_t[...], L[:, cols], preferred_element_type=F32)
        inv = sw_inv[:, cols]
        inner = jnp.sum(sw_bf[:, cols].astype(F32) * g, axis=0, keepdims=True)
        g = (g - sw_raw[:, cols].astype(F32) * (inv * inner)) * inv
        G[q] = g.reshape(NY, NZ, 8, QUARTER)

    def steps(q, way):
        return NZ // 2 if (q < 2) == (way == 1) else NZ // 2 - 1

    def ring(q, k, way):
        buf, send, recv = (ring_r, rr_send, rr_recv) if way == 1 else (ring_l, rl_send, rl_recv)
        if k >= steps(q, way):
            return
        dest = (z + way * (steps(q, way) - k) + NZ) % NZ
        if k == 0:
            src = G.at[q, :, dest]
        else:
            wait_bytes(buf.at[q, k - 1], recv.at[q, k - 1])
            buf[q, k - 1] = buf[q, k - 1] + G[q, :, dest]
            src = buf.at[q, k - 1]
        remote(src, buf.at[q, k], send.at[q, k], recv.at[q, k], dev(0, way, 0, 0)).start()

    def turned_rows(core_of, x_of, count):
        return pl.ds(pl.multiple_of((core_of * NX + x_of) * 32, 32), 32 * count)

    def h_block(b):
        rows = slice(b * ROWS, (b + 1) * ROWS)
        A[rows, 0:D] = jnp.dot(L[rows, :], sw_t[...], preferred_element_type=F32)

    def h_finish():
        def one(b, carry):
            rows = pl.ds(pl.multiple_of(b * 128, 128), 128)
            h = A[rows, 0:D]
            inner = jnp.sum(s_bf[rows, :].astype(F32) * h, axis=1, keepdims=True)
            inv = jnp.concatenate([s_inv[rows, :]] * 2, axis=1)
            h = (h - s_raw[rows, :].astype(F32) * inv * inner) * inv
            turned = h.T
            for p in range(NX * NC):
                E[turned_rows(p % NC, p // NC, 1), rows] = turned[p * 32:(p + 1) * 32, :]
            return carry

        lax.fori_loop(0, BLOCKS, one, 0)

    core = remote(E.at[turned_rows(1 - c, 0, NX), 0:TILE_ROWS], h_core, hc_send, hc_recv, dev(0, 0, 0, 1))

    def h_spread():
        core.wait_recv()

        def add(i, carry):
            here = turned_rows(c, i, 1)
            E[here, 0:TILE_ROWS] = E[here, 0:TILE_ROWS] + h_core[pl.ds(pl.multiple_of(i * 32, 32), 32), :]
            return carry

        lax.fori_loop(0, NX, add, 0)
        for i, (dy, dx) in enumerate(sheet):
            to_y, to_x = (y + dy) % NY, (x + dx) % NX
            remote(
                E.at[turned_rows(c, to_x, 1), block_rows(to_y)], h_in.at[i], h_send, h_recv, dev(dy, 0, dx, 0)
            ).start()

    def h_done():
        wait_bytes(h_in, h_recv)
        total = E[turned_rows(c, x, 1), block_rows(y)]
        for i in range(len(sheet)):
            total = total + h_in[i]
        hout_ref[...] = total

    between = [
        lambda: (h_block(0), h_block(1)), lambda: (h_block(2), h_block(3)), lambda: (h_finish(), core.start()),
        lambda: None, h_spread,
    ]

    for q in range(4):
        quarter(q)
        ring(q, 0, 1)
        ring(q, 0, -1)
    for k in range(1, NZ // 2):
        for q in range(4):
            ring(q, k, 1)
            ring(q, k, -1)
            if between:
                between.pop(0)()

    for q in range(4):
        last_r, last_l = steps(q, 1) - 1, steps(q, -1) - 1
        wait_bytes(ring_r.at[q, last_r], rr_recv.at[q, last_r])
        wait_bytes(ring_l.at[q, last_l], rl_recv.at[q, last_l])
        g_sum[q] = G[q, :, z] + ring_r[q, last_r] + ring_l[q, last_l]
        for o in (2, 1, 3):
            remote(
                g_sum.at[q, (y + o) % NY], g_out.at[q, o - 1], a_send.at[q], a_recv.at[q], dev(o, 0, 0, 0)
            ).start()
        wout_ref[:, pl.ds(pl.multiple_of(y * TILE_COLS + q * QUARTER, QUARTER), QUARTER)] = g_sum[q, y]
    h_done()
    for q in range(4):
        wait_bytes(g_out.at[q], a_recv.at[q])
        for o in range(1, NY):
            at = pl.multiple_of(((y + NY - o) % NY) * TILE_COLS + q * QUARTER, QUARTER)
            wout_ref[:, pl.ds(at, QUARTER)] = g_out[q, o - 1]

    for buf, send, fsend in ((t_in, t_send, t_fsend), (s_in, s_send, s_fsend)):
        wait_bytes(buf.at[:, 0], send)
        wait_bytes(buf.at[:, 0], fsend)
    wait_bytes(y_in, y_send)
    for r in range(BALANCE_STEPS):
        for half in range(2):
            wait_bytes(c_in.at[r, half], c_send.at[r, half])
    for r in range(BALANCE_STEPS + 1):
        wait_bytes(r_in.at[r], r_send.at[r])
    for q in range(4):
        for k in range(steps(q, 1)):
            wait_bytes(ring_r.at[q, k], rr_send.at[q, k])
        for k in range(steps(q, -1)):
            wait_bytes(ring_l.at[q, k], rl_send.at[q, k])
        wait_bytes(g_out.at[q], a_send.at[q])
    core.wait_send()
    wait_bytes(h_in, h_send)


def shards(student_features, teacher_features, student_weight, teacher_weight):
    crops_all = student_features.shape[0] * lax.axis_size("crop")
    factor = LOSS_SCALE / (STUDENT_TEMP * crops_all)
    vmem = pl.BlockSpec(memory_space=pltpu.VMEM)
    hbm = pl.BlockSpec(memory_space=pl.ANY)
    far_memory = pl.BlockSpec(memory_space=pltpu.HBM)
    peers, sheet = NY * NX * NC - 1, NY * NX - 1
    v = pltpu.VMEM
    dma = pltpu.SemaphoreType.DMA
    scratch = [
        v((TILE_ROWS, TILE_COLS), F32), v((TILE_ROWS, TILE_COLS), F32),
        v((D, TILE_COLS), BF16), v((D, TILE_COLS), BF16),
        v((D, TILE_COLS), BF16), v((D, TILE_COLS), BF16),
        v((TILE_COLS, D), BF16), v((1, TILE_COLS), F32),
        v((TILE_ROWS, D), BF16), v((TILE_ROWS, D), BF16), v((D, TILE_ROWS), BF16),
        v((TILE_ROWS, D), BF16), v((TILE_ROWS, 128), F32),
        v((TILE_ROWS, 128), F32), v((TILE_ROWS, 128), F32),
        v((2, 2, PIECE, D), F32), v((2, 2, PIECE, D), F32),
        v((NY - 1, 2, 2, PIECE, D), F32), v((NY - 1, 2, 2, PIECE, D), F32),
        v((1, TILE_COLS), F32), v((NY - 1, 1, TILE_COLS), F32), v((NY - 1, 1, TILE_COLS), F32),
        v((BALANCE_STEPS, 2, 1, HALF), F32), v((BALANCE_STEPS, 2, NZ - 1, 1, HALF), F32),
        v((BALANCE_STEPS + 1, BLOCKS, 128), F32), v((BALANCE_STEPS + 1, peers, BLOCKS, 128), F32),
        v((16, 128), F32),
        v((TILE_ROWS, TILE_COLS), BF16),
        v((4, NY, NZ, 8, QUARTER), F32),
        v((4, NZ // 2, NY, 8, QUARTER), F32), v((4, NZ // 2, NY, 8, QUARTER), F32),
        v((4, NY, 8, QUARTER), F32), v((4, NY - 1, 8, QUARTER), F32),
        v((NX * 32, TILE_ROWS), F32), v((sheet, 32, ROWS), F32),
        dma((5,)), dma, dma((3,)),
        dma, dma((3, 2)), dma, dma((3, 2)),
        dma, dma((3, 2)), dma, dma((3, 2)),
        dma((3, 2)), dma((3, 2)), dma((4,)), dma((4,)),
        dma((4, 4)), dma((4, 4)), dma((4, 4)), dma((4, 4)),
        dma((4,)), dma((4,)), dma, dma, dma, dma,
    ]
    weight_grad, turned = pl.pallas_call(
        functools.partial(kernel, factor),
        out_shape=(
            jax.ShapeDtypeStruct((D // (NY * NZ), NY * TILE_COLS), F32),
            jax.ShapeDtypeStruct((D // (NX * NC), ROWS), F32),
        ),
        in_specs=[vmem, vmem, hbm, hbm],
        out_specs=(vmem, vmem),
        scratch_shapes=scratch,
        compiler_params=pltpu.CompilerParams(
            collective_id=0, has_side_effects=True, vmem_limit_bytes=53 * 1024 * 1024
        ),
        name="prototype_head",
    )(teacher_features, student_features, teacher_weight, student_weight)
    def hand_over(a_ref, b_ref, a_out, b_out, sem):
        copies = [
            pltpu.make_async_copy(a_ref, a_out, sem.at[0]),
            pltpu.make_async_copy(b_ref, b_out, sem.at[1]),
        ]
        for copy in copies:
            copy.start()
        for copy in copies:
            copy.wait()

    weight_grad, turned = pl.pallas_call(
        hand_over,
        out_shape=(
            jax.ShapeDtypeStruct(weight_grad.shape, F32),
            jax.ShapeDtypeStruct(turned.shape, F32),
        ),
        in_specs=[vmem, vmem],
        out_specs=(far_memory, far_memory),
        scratch_shapes=[dma((2,))],
        compiler_params=pltpu.CompilerParams(vmem_limit_bytes=2 * 1024 * 1024),
        name="hand_over",
    )(weight_grad, turned)
    return weight_grad, turned.T


def solution(mesh):
    return jax.shard_map(
        shards,
        mesh=mesh,
        in_specs=(P("crop", None), P("crop", None), P(None, "proto"), P(None, "proto")),
        out_specs=(P("crop", "proto"), P("crop", "proto")),
        check_vma=False,
    )
```

```python
import functools
import math

import jax
import jax.numpy as jnp
from jax import lax
from jax.experimental import pallas as pl
from jax.experimental.pallas import tpu as pltpu
from jax.sharding import PartitionSpec as P

BALANCE_STEPS = 3
LOSS_SCALE = 4194304
EPSILON = 1e-06
TEACHER_TEMP = 0.07
STUDENT_TEMP = 0.1
LOG2E = math.log2(math.e)

NY, NZ, NX, NC = 4, 8, 4, 2
D = 256
ROWS = 384
TILE_ROWS = NY * ROWS
TILE_COLS = 2048
HALF = TILE_COLS // 2
QUARTER = TILE_COLS // 4
BLOCKS = TILE_ROWS // 128
PIECE = ROWS // 4
MESH = pl.DeviceIdType.MESH
F32, BF16 = jnp.float32, jnp.bfloat16


def kernel(
    factor,
    t_ref, s_ref, tw_hbm, sw_hbm,
    wout_ref, hout_ref,
    E, A, tw_raw, sw_raw, tw_bf, sw_bf, sw_t, sw_inv, t_bf, s_bf, s_t, s_raw, s_inv,
    u_wide, part, t_src, s_src, t_in, s_in,
    y_own, y_src, y_in, c_src, c_in, r_src, r_in, flat_ref,
    L, G, ring_r, ring_l, g_sum, g_out, h_core, h_in,
    load_sem, y_send, y_recv, t_send, t_recv, t_fsend, t_frecv, s_send, s_recv, s_fsend, s_frecv,
    c_send, c_recv, r_send, r_recv,
    rr_send, rr_recv, rl_send, rl_recv, a_send, a_recv, hc_send, hc_recv, h_send, h_recv,
):
    crop, proto = lax.axis_index("crop"), lax.axis_index("proto")
    y, z, x, c = crop // NZ, crop % NZ, proto // NC, proto % NC

    def dev(dy, dz, dx, dc):
        return (((y + dy) % NY) * NZ + (z + dz) % NZ, ((x + dx) % NX) * NC + (c + dc) % NC)

    def remote(src, dst, send, recv, to):
        return pltpu.make_async_remote_copy(
            src_ref=src, dst_ref=dst, send_sem=send, recv_sem=recv, device_id=to, device_id_type=MESH
        )

    def wait_bytes(buf, sem):
        pltpu.make_async_copy(buf, buf, sem).wait()

    def far(d, n):
        return min(d, n - d)

    plane = sorted(
        ((dy, dx, dc) for dy in range(NY) for dx in range(NX) for dc in range(NC) if (dy, dx, dc) != (0, 0, 0)),
        key=lambda o: -(far(o[0], NY) + far(o[1], NX)),
    )
    sheet = sorted(
        ((dy, dx) for dy in range(NY) for dx in range(NX) if (dy, dx) != (0, 0)),
        key=lambda o: -(far(o[0], NY) + far(o[1], NX)),
    )
    line = sorted(range(1, NZ), key=lambda d: -far(d, NZ))

    barrier = pltpu.get_barrier_semaphore()
    for dy, dx, dc in plane:
        pl.semaphore_signal(barrier, inc=1, device_id=dev(dy, 0, dx, dc), device_id_type=MESH)
    for dz in line:
        pl.semaphore_signal(barrier, inc=1, device_id=dev(0, dz, 0, 0), device_id_type=MESH)

    col0 = pl.multiple_of(y * TILE_COLS, TILE_COLS)
    load_t = pltpu.make_async_copy(tw_hbm.at[:, pl.ds(col0, TILE_COLS)], tw_raw, load_sem.at[0])
    load_s = pltpu.make_async_copy(sw_hbm.at[:, pl.ds(col0, TILE_COLS)], sw_raw, load_sem.at[1])
    loads = {}
    for o in (2, 1, 3):
        col = pl.multiple_of(((y + o) % NY) * TILE_COLS, TILE_COLS)
        loads[o] = pltpu.make_async_copy(
            tw_hbm.at[:, pl.ds(col, TILE_COLS)], L.at[(o - 1) * D:o * D, :], load_sem.at[1 + o]
        )
        loads[o].start()
    load_t.start()
    load_s.start()

    def block_rows(block):
        return pl.ds(pl.multiple_of(block * ROWS, ROWS), ROWS)

    def normalise(raw, out, inv_ref):
        def one(q, carry):
            cols = pl.ds(pl.multiple_of(q * QUARTER, QUARTER), QUARTER)
            w = raw[:, cols].astype(F32)
            inv = 1.0 / jnp.sqrt(jnp.sum(w * w, axis=0, keepdims=True) + EPSILON)
            out[:, cols] = (w * inv).astype(BF16)
            if inv_ref is not None:
                inv_ref[:, cols] = inv
            return carry

        lax.fori_loop(0, 4, one, 0)

    t32 = t_ref[...].astype(F32)
    t_own = (t32 * (1.0 / jnp.sqrt(jnp.sum(t32 * t32, axis=1, keepdims=True) + EPSILON))).astype(BF16)
    t_bf[block_rows(y), :] = t_own
    t_src[...] = t_own.astype(F32).reshape(2, 2, PIECE, D)
    s_src[...] = s_ref[...].astype(F32).reshape(2, 2, PIECE, D)

    pl.semaphore_wait(barrier, len(plane) + NZ - 1)

    def gather_start(src, dst, send, recv):
        for piece, way in ((0, 1), (1, 3), (1, 1), (0, 3)):
            remote(src.at[c, piece], dst.at[way - 1, c, piece], send, recv.at[way - 1, piece], dev(way, 0, 0, 0)).start()

    def gather_relay(dst, send, recv):
        for piece, way in ((0, 1), (1, 3)):
            wait_bytes(dst.at[way - 1, c, piece], recv.at[way - 1, piece])
            remote(
                dst.at[way - 1, c, piece], dst.at[1, c, piece], send, recv.at[1, piece], dev(way, 0, 0, 0)
            ).start()

    def gather_core(dst, fsend, frecv, way, piece):
        remote(
            dst.at[way - 1, c, piece], dst.at[way - 1, c, piece], fsend, frecv.at[way - 1, piece], dev(0, 0, 0, 1)
        ).start()

    def gather_near(dst, recv, fsend, frecv):
        gather_core(dst, fsend, frecv, 1, 0)
        gather_core(dst, fsend, frecv, 3, 1)
        for piece, way in ((1, 1), (0, 3)):
            wait_bytes(dst.at[way - 1, c, piece], recv.at[way - 1, piece])
            gather_core(dst, fsend, frecv, way, piece)

    def gather_far(dst, recv, fsend, frecv):
        for piece in range(2):
            wait_bytes(dst.at[1, c, piece], recv.at[1, piece])
            gather_core(dst, fsend, frecv, 2, piece)

    def gather_done(dst, frecv, way):
        for piece in range(2):
            wait_bytes(dst.at[way - 1, 1 - c, piece], frecv.at[way - 1, piece])
        return (y + NY - way) % NY, dst[way - 1].reshape(ROWS, D)

    def cols_start(r, half, sums):
        c_src[r, half] = jnp.sum(sums, axis=0, keepdims=True)
        for i, dz in enumerate(line):
            remote(
                c_src.at[r, half], c_in.at[r, half, i], c_send.at[r, half], c_recv.at[r, half], dev(0, dz, 0, 0)
            ).start()

    def cols_done(r, half):
        wait_bytes(c_in.at[r, half], c_recv.at[r, half])
        total = c_src[r, half]
        for i in range(len(line)):
            total = total + c_in[r, half, i]
        return 1.0 / total

    gather_start(t_src, t_in, t_send, t_recv)

    def teacher_exp(rows, weight, cols):
        return jnp.exp2(jnp.dot(t_bf[rows, :], weight[:, cols], preferred_element_type=F32) * (LOG2E / TEACHER_TEMP))

    def halves(one):
        def step(half, carry):
            one(pl.ds(pl.multiple_of(half * HALF, HALF), HALF))
            return carry

        lax.fori_loop(0, 2, step, 0)

    def exp_block(block):
        rows = block_rows(block)

        def one(cols):
            E[rows, cols] = teacher_exp(rows, tw_bf, cols)

        halves(one)

    def own_sums(weight, dst, keep):
        rows = block_rows(y)

        def one(cols):
            e = teacher_exp(rows, weight, cols)
            if keep:
                E[rows, cols] = e
            sums = jnp.sum(e.reshape(ROWS // 8, 8, HALF), axis=0)
            dst[:, cols] = jnp.sum(sums, axis=0, keepdims=True)

        halves(one)

    def sums_for(o):
        loads[o].wait()
        weight = L.at[(NY + o - 2) * D:(NY + o - 1) * D, :]
        normalise(L.at[(o - 1) * D:o * D, :], weight, None)
        own_sums(weight, y_src.at[o - 1], False)
        remote(y_src.at[o - 1], y_in.at[o - 1], y_send, y_recv.at[o - 1], dev(o, 0, 0, 0)).start()

    sums_for(2)
    sums_for(1)
    sums_for(3)
    load_t.wait()
    normalise(tw_raw, tw_bf, None)
    own_sums(tw_bf, y_own, True)
    gather_relay(t_in, t_send, t_recv)
    gather_near(t_in, t_recv, t_fsend, t_frecv)
    for o in range(1, NY):
        wait_bytes(y_in.at[o - 1], y_recv.at[o - 1])
    col_sums = y_own[...] + y_in[0] + y_in[1] + y_in[2]
    cols_start(0, 0, col_sums[:, :HALF])
    cols_start(0, 1, col_sums[:, HALF:])
    for way in (1, 3, 2):
        if way == 3:
            gather_far(t_in, t_recv, t_fsend, t_frecv)
        block, rows = gather_done(t_in, t_frecv, way)
        t_bf[block_rows(block), :] = rows.astype(BF16)
        exp_block(block)
    gather_start(s_src, s_in, s_send, s_recv)

    lane = lax.broadcasted_iota(jnp.int32, (8, 128), 1)
    sublane = lax.broadcasted_iota(jnp.int32, (8, 128), 0)

    def rows_of(src, r, scaled, store):
        for half in range(2):
            scale = cols_done(r, half) if scaled else None

            def one(b, carry):
                rows = pl.ds(pl.multiple_of(b * 128, 128), 128)
                acc = part[rows, :] if half else None
                for k in range(HALF // 128):
                    cols = slice(half * HALF + k * 128, half * HALF + (k + 1) * 128)
                    term = src[rows, cols]
                    if scaled:
                        term = term * scale[:, k * 128:(k + 1) * 128]
                    if store:
                        src[rows, cols] = term
                    acc = term if acc is None else acc + term
                part[rows, :] = acc
                return carry

            lax.fori_loop(0, BLOCKS, one, 0)

        def packed(g0, g1):
            out = None
            for base in range(g0, g1, 16):
                some = jnp.zeros((8, 128), F32)
                for g in range(base, base + 16):
                    total = jnp.sum(part[8 * g:8 * g + 8, :], axis=1, keepdims=True)
                    some = jnp.where(lane == g - g0, total, some)
                out = some if out is None else out + some
            return out

        r_src[r, 0:8, :] = packed(0, 128)
        rest = packed(128, 192)
        rest = rest + pltpu.roll(pltpu.roll(rest, 64, 1), 4, 0)
        r_src[r, 8:12, :] = rest[0:4, :]

    def rows_start(r):
        for i, (dy, dx, dc) in enumerate(plane):
            remote(r_src.at[r], r_in.at[r, i], r_send.at[r], r_recv.at[r], dev(dy, 0, dx, dc)).start()

    def rows_done(r, dst, scale):
        wait_bytes(r_in.at[r], r_recv.at[r])
        total = r_src[r]
        for i in range(len(plane)):
            total = total + r_in[r, i]
        flat_ref[0:BLOCKS, :] = scale / total
        low, rest = flat_ref[0:8, :], flat_ref[8:16, :]
        high = jnp.where(sublane < 4, rest, pltpu.roll(pltpu.roll(rest, 64, 1), 4, 0))
        for g in range(TILE_ROWS // 8):
            value = low[:, g:g + 1] if g < 128 else high[:, g - 128:g - 127]
            dst[8 * g:8 * g + 8, :] = jnp.broadcast_to(value, (8, 128))

    def cols_of(r):
        for half in range(2):

            def one(b, acc):
                rows = pl.ds(pl.multiple_of(b * 128, 128), 128)
                u = u_wide[rows, :]
                out = []
                for k in range(HALF // 128):
                    e = E[rows, half * HALF + k * 128:half * HALF + (k + 1) * 128] * u
                    out.append(acc[k] + jnp.sum(e.reshape(16, 8, 128), axis=0))
                return tuple(out)

            zero = tuple(jnp.zeros((8, 128), F32) for _ in range(HALF // 128))
            cols_start(r, half, jnp.concatenate(lax.fori_loop(0, BLOCKS, one, zero), axis=1))

    def student_exp():
        def one(i, carry):
            rows = pl.ds(pl.multiple_of((i // 2) * ROWS, ROWS), ROWS)
            cols = pl.ds(pl.multiple_of((i % 2) * HALF, HALF), HALF)
            A[rows, cols] = jnp.exp2(
                jnp.dot(s_bf[rows, :], sw_bf[:, cols], preferred_element_type=F32) * (LOG2E / STUDENT_TEMP)
            )
            return carry

        lax.fori_loop(0, 2 * NY, one, 0)

    def student_block(block, raw):
        inv = 1.0 / jnp.sqrt(jnp.sum(raw * raw, axis=1, keepdims=True) + EPSILON)
        unit = raw * inv
        rows = block_rows(block)
        s_raw[rows, :] = raw.astype(BF16)
        s_inv[rows, :] = jnp.broadcast_to(inv, (ROWS, 128))
        s_bf[rows, :] = unit.astype(BF16)

    rows_of(E, 0, True, False)
    rows_start(0)
    load_s.wait()
    normalise(sw_raw, sw_bf, sw_inv)
    for q in range(4):
        sw_t[q * QUARTER:(q + 1) * QUARTER, :] = sw_bf[:, q * QUARTER:(q + 1) * QUARTER].T
    student_block(y, s_src[...].reshape(ROWS, D))
    gather_relay(s_in, s_send, s_recv)
    rows_done(0, u_wide, 1.0)
    cols_of(1)
    gather_near(s_in, s_recv, s_fsend, s_frecv)
    gather_far(s_in, s_recv, s_fsend, s_frecv)
    for way in (1, 3, 2):
        student_block(*gather_done(s_in, s_frecv, way))
    rows_of(E, 1, True, False)
    rows_start(1)
    student_exp()
    rows_done(1, u_wide, 1.0)
    cols_of(2)
    rows_of(A, 3, False, False)
    rows_start(3)
    rows_of(E, 2, True, True)
    rows_start(2)
    for b in range(BLOCKS):
        s_t[:, b * 128:(b + 1) * 128] = s_bf[b * 128:(b + 1) * 128, :].T
    z_wide = part
    rows_done(3, z_wide, factor)

    def probs(b, carry):
        rows = pl.ds(pl.multiple_of(b * 128, 128), 128)
        w = z_wide[rows, :]
        for k in range(TILE_COLS // 128):
            A[rows, k * 128:(k + 1) * 128] = A[rows, k * 128:(k + 1) * 128] * w
        return carry

    lax.fori_loop(0, BLOCKS, probs, 0)
    rows_done(2, u_wide, factor)

    def quarter(q):
        lo = q * QUARTER

        def one(b, carry):
            rows = pl.ds(pl.multiple_of(b * 128, 128), 128)
            u = u_wide[rows, :]
            for k in range(QUARTER // 128):
                at = slice(lo + k * 128, lo + (k + 1) * 128)
                L[rows, at] = (A[rows, at] - E[rows, at] * u).astype(BF16)
            return carry

        lax.fori_loop(0, BLOCKS, one, 0)
        cols = slice(lo, lo + QUARTER)
        g = jnp.dot(s_t[...], L[:, cols], preferred_element_type=F32)
        inv = sw_inv[:, cols]
        inner = jnp.sum(sw_bf[:, cols].astype(F32) * g, axis=0, keepdims=True)
        g = (g - sw_raw[:, cols].astype(F32) * (inv * inner)) * inv
        G[q] = g.reshape(NY, NZ, 8, QUARTER)

    def steps(q, way):
        return NZ // 2 if (q < 2) == (way == 1) else NZ // 2 - 1

    def ring(q, k, way):
        buf, send, recv = (ring_r, rr_send, rr_recv) if way == 1 else (ring_l, rl_send, rl_recv)
        if k >= steps(q, way):
            return
        dest = (z + way * (steps(q, way) - k) + NZ) % NZ
        if k == 0:
            src = G.at[q, :, dest]
        else:
            wait_bytes(buf.at[q, k - 1], recv.at[q, k - 1])
            buf[q, k - 1] = buf[q, k - 1] + G[q, :, dest]
            src = buf.at[q, k - 1]
        remote(src, buf.at[q, k], send.at[q, k], recv.at[q, k], dev(0, way, 0, 0)).start()

    def turned_rows(core_of, x_of, count):
        return pl.ds(pl.multiple_of((core_of * NX + x_of) * 32, 32), 32 * count)

    def h_block(b):
        rows = slice(b * ROWS, (b + 1) * ROWS)
        A[rows, 0:D] = jnp.dot(L[rows, :], sw_t[...], preferred_element_type=F32)

    def h_finish():
        def one(b, carry):
            rows = pl.ds(pl.multiple_of(b * 128, 128), 128)
            h = A[rows, 0:D]
            inner = jnp.sum(s_bf[rows, :].astype(F32) * h, axis=1, keepdims=True)
            inv = jnp.concatenate([s_inv[rows, :]] * 2, axis=1)
            h = (h - s_raw[rows, :].astype(F32) * inv * inner) * inv
            turned = h.T
            for p in range(NX * NC):
                E[turned_rows(p % NC, p // NC, 1), rows] = turned[p * 32:(p + 1) * 32, :]
            return carry

        lax.fori_loop(0, BLOCKS, one, 0)

    core = remote(E.at[turned_rows(1 - c, 0, NX), 0:TILE_ROWS], h_core, hc_send, hc_recv, dev(0, 0, 0, 1))

    def h_spread():
        core.wait_recv()

        def add(i, carry):
            here = turned_rows(c, i, 1)
            E[here, 0:TILE_ROWS] = E[here, 0:TILE_ROWS] + h_core[pl.ds(pl.multiple_of(i * 32, 32), 32), :]
            return carry

        lax.fori_loop(0, NX, add, 0)
        for i, (dy, dx) in enumerate(sheet):
            to_y, to_x = (y + dy) % NY, (x + dx) % NX
            remote(
                E.at[turned_rows(c, to_x, 1), block_rows(to_y)], h_in.at[i], h_send, h_recv, dev(dy, 0, dx, 0)
            ).start()

    def h_done():
        wait_bytes(h_in, h_recv)
        total = E[turned_rows(c, x, 1), block_rows(y)]
        for i in range(len(sheet)):
            total = total + h_in[i]
        hout_ref[...] = total

    between = [
        lambda: (h_block(0), h_block(1)), lambda: (h_block(2), h_block(3)), lambda: (h_finish(), core.start()),
        lambda: None, h_spread,
    ]

    for q in range(4):
        quarter(q)
        ring(q, 0, 1)
        ring(q, 0, -1)
    for k in range(1, NZ // 2):
        for q in range(4):
            ring(q, k, 1)
            ring(q, k, -1)
            if between:
                between.pop(0)()

    for q in range(4):
        last_r, last_l = steps(q, 1) - 1, steps(q, -1) - 1
        wait_bytes(ring_r.at[q, last_r], rr_recv.at[q, last_r])
        wait_bytes(ring_l.at[q, last_l], rl_recv.at[q, last_l])
        g_sum[q] = G[q, :, z] + ring_r[q, last_r] + ring_l[q, last_l]
        for o in (2, 1, 3):
            remote(
                g_sum.at[q, (y + o) % NY], g_out.at[q, o - 1], a_send.at[q], a_recv.at[q], dev(o, 0, 0, 0)
            ).start()
        wout_ref[:, pl.ds(pl.multiple_of(y * TILE_COLS + q * QUARTER, QUARTER), QUARTER)] = g_sum[q, y]
    h_done()
    for q in range(4):
        wait_bytes(g_out.at[q], a_recv.at[q])
        for o in range(1, NY):
            at = pl.multiple_of(((y + NY - o) % NY) * TILE_COLS + q * QUARTER, QUARTER)
            wout_ref[:, pl.ds(at, QUARTER)] = g_out[q, o - 1]

    for buf, send, fsend in ((t_in, t_send, t_fsend), (s_in, s_send, s_fsend)):
        wait_bytes(buf.at[:, 0], send)
        wait_bytes(buf.at[:, 0], fsend)
    wait_bytes(y_in, y_send)
    for r in range(BALANCE_STEPS):
        for half in range(2):
            wait_bytes(c_in.at[r, half], c_send.at[r, half])
    for r in range(BALANCE_STEPS + 1):
        wait_bytes(r_in.at[r], r_send.at[r])
    for q in range(4):
        for k in range(steps(q, 1)):
            wait_bytes(ring_r.at[q, k], rr_send.at[q, k])
        for k in range(steps(q, -1)):
            wait_bytes(ring_l.at[q, k], rl_send.at[q, k])
        wait_bytes(g_out.at[q], a_send.at[q])
    core.wait_send()
    wait_bytes(h_in, h_send)


def shards(student_features, teacher_features, student_weight, teacher_weight):
    crops_all = student_features.shape[0] * lax.axis_size("crop")
    factor = LOSS_SCALE / (STUDENT_TEMP * crops_all)
    vmem = pl.BlockSpec(memory_space=pltpu.VMEM)
    hbm = pl.BlockSpec(memory_space=pl.ANY)
    far_memory = pl.BlockSpec(memory_space=pltpu.HBM)
    peers, sheet = NY * NX * NC - 1, NY * NX - 1
    v = pltpu.VMEM
    dma = pltpu.SemaphoreType.DMA
    scratch = [
        v((TILE_ROWS, TILE_COLS), F32), v((TILE_ROWS, TILE_COLS), F32),
        v((D, TILE_COLS), BF16), v((D, TILE_COLS), BF16),
        v((D, TILE_COLS), BF16), v((D, TILE_COLS), BF16),
        v((TILE_COLS, D), BF16), v((1, TILE_COLS), F32),
        v((TILE_ROWS, D), BF16), v((TILE_ROWS, D), BF16), v((D, TILE_ROWS), BF16),
        v((TILE_ROWS, D), BF16), v((TILE_ROWS, 128), F32),
        v((TILE_ROWS, 128), F32), v((TILE_ROWS, 128), F32),
        v((2, 2, PIECE, D), F32), v((2, 2, PIECE, D), F32),
        v((NY - 1, 2, 2, PIECE, D), F32), v((NY - 1, 2, 2, PIECE, D), F32),
        v((1, TILE_COLS), F32), v((NY - 1, 1, TILE_COLS), F32), v((NY - 1, 1, TILE_COLS), F32),
        v((BALANCE_STEPS, 2, 1, HALF), F32), v((BALANCE_STEPS, 2, NZ - 1, 1, HALF), F32),
        v((BALANCE_STEPS + 1, BLOCKS, 128), F32), v((BALANCE_STEPS + 1, peers, BLOCKS, 128), F32),
        v((16, 128), F32),
        v((TILE_ROWS, TILE_COLS), BF16),
        v((4, NY, NZ, 8, QUARTER), F32),
        v((4, NZ // 2, NY, 8, QUARTER), F32), v((4, NZ // 2, NY, 8, QUARTER), F32),
        v((4, NY, 8, QUARTER), F32), v((4, NY - 1, 8, QUARTER), F32),
        v((NX * 32, TILE_ROWS), F32), v((sheet, 32, ROWS), F32),
        dma((5,)), dma, dma((3,)),
        dma, dma((3, 2)), dma, dma((3, 2)),
        dma, dma((3, 2)), dma, dma((3, 2)),
        dma((3, 2)), dma((3, 2)), dma((4,)), dma((4,)),
        dma((4, 4)), dma((4, 4)), dma((4, 4)), dma((4, 4)),
        dma((4,)), dma((4,)), dma, dma, dma, dma,
    ]
    weight_grad, turned = pl.pallas_call(
        functools.partial(kernel, factor),
        out_shape=(
            jax.ShapeDtypeStruct((D // (NY * NZ), NY * TILE_COLS), F32),
            jax.ShapeDtypeStruct((D // (NX * NC), ROWS), F32),
        ),
        in_specs=[vmem, vmem, hbm, hbm],
        out_specs=(vmem, vmem),
        scratch_shapes=scratch,
        compiler_params=pltpu.CompilerParams(
            collective_id=0, has_side_effects=True, vmem_limit_bytes=53 * 1024 * 1024
        ),
        name="prototype_head",
    )(teacher_features, student_features, teacher_weight, student_weight)
    def hand_over(a_ref, b_ref, a_out, b_out, sem):
        copies = [
            pltpu.make_async_copy(a_ref, a_out, sem.at[0]),
            pltpu.make_async_copy(b_ref, b_out, sem.at[1]),
        ]
        for copy in copies:
            copy.start()
        for copy in copies:
            copy.wait()

    weight_grad, turned = pl.pallas_call(
        hand_over,
        out_shape=(
            jax.ShapeDtypeStruct(weight_grad.shape, F32),
            jax.ShapeDtypeStruct(turned.shape, F32),
        ),
        in_specs=[vmem, vmem],
        out_specs=(far_memory, far_memory),
        scratch_shapes=[dma((2,))],
        compiler_params=pltpu.CompilerParams(vmem_limit_bytes=2 * 1024 * 1024),
        name="hand_over",
    )(weight_grad, turned)
    return weight_grad, turned.T


def solution(mesh):
    return jax.shard_map(
        shards,
        mesh=mesh,
        in_specs=(P("crop", None), P("crop", None), P(None, "proto"), P(None, "proto")),
        out_specs=(P("crop", "proto"), P("crop", "proto")),
        check_vma=False,
    )
```
